128 devices in a mesh: row: 8 (over y, z_lo), col: 16 (over z_hi, x, core).
Axes of the slice: x: 4, y: 4, z: 4 (z_hi: 2, z_lo: 2; z = z_hi * 2 + z_lo), core: 2. Of those that a mesh axis runs over, the one named last changes fastest.
Arguments:
- velocities: bfloat16 [1024, 61440], P(None, 'row'), may hold values from -60 to 60, as said below
- modes_panel: bfloat16 [61440, 4096], P('row', 'col'), may hold values from -1 to 1
- atom_slot: int32 [20480], P('row'), may hold values from 0 to 2559, as said below
- lag_offsets: int32 [8], replicated, may hold values from 0 to 256, as said below
Outputs:
- correlations: float32 [8, 4096, 4096], P(None, 'row', 'col')
The draws below stay inside these ranges and needn't reach their ends.
Inputs may be any that keep to these rules, and one draw needn't show every extreme that they name: `velocities`: every snapshot row has its own scale. Within each aligned block of 2560 atoms, atom_slot is a permutation of 0 to 2559. `lag_offsets`: one of the lags equals 256.
All inputs are finite; a program needn't handle non-finite values.
Results may differ from the reference program's by a relative error of at most 0.0041.
Values may be sent and summed in bfloat16 or wider, within the bound.
A program may use at most 128 MiB of HBM per device.

```python
import jax
import jax.numpy as jnp
from jax import lax

M = 4096
ATOM_DEV = 2560
S = 1024
LAGS = 8
NATOMS = 20480
COORDS = 61440
MAXLAG = 256


def draw_velocities(key, part):
    first, second = jax.random.split(jax.random.fold_in(key, 11))
    base = jnp.clip(jax.random.normal(first, (S, COORDS), jnp.float32), -6.0, 6.0)
    scales = jnp.exp(jax.random.uniform(second, (S, 1), jnp.float32, 0.0, jnp.log(10.0)))
    return jnp.clip(base * scales, -60.0, 60.0).astype(jnp.bfloat16)


def draw_modes_panel(key, part):
    first, second = jax.random.split(jax.random.fold_in(key, 23))
    ramp = jnp.arange(M, dtype=jnp.float32) / (M - 1)
    base = jnp.clip(jax.random.normal(first, (COORDS, M), jnp.float32), -6.0, 6.0)
    scales = jnp.exp(jnp.log(3.0) * ramp) * jax.random.uniform(second, (M,), jnp.float32, 0.7, 1.4)
    values = base * scales[None, :] * (1.0 / jnp.sqrt(jnp.float32(COORDS)))
    return jnp.clip(values, -1.0, 1.0).astype(jnp.bfloat16)


def draw_atom_slot(key, part):
    keys = jax.random.split(jax.random.fold_in(key, 37), NATOMS // ATOM_DEV)
    perms = jax.vmap(lambda single: jax.random.permutation(single, ATOM_DEV))(keys)
    return perms.reshape(NATOMS).astype(jnp.int32)


def draw_lag_offsets(key, part):
    first, second = jax.random.split(jax.random.fold_in(key, 41))
    values = jax.random.randint(first, (LAGS,), 0, MAXLAG, jnp.int32)
    where_top = jax.random.randint(second, (), 0, LAGS, jnp.int32)
    return jnp.where(jnp.arange(LAGS, dtype=jnp.int32) == where_top, MAXLAG, values).astype(jnp.int32)


def setup_inputs(seed: int = 0) -> dict:
    splits = jax.random.split(jax.random.key(seed), 5)
    velocities = draw_velocities(jax.random.fold_in(splits[4], 71), 0)
    modes_panel = draw_modes_panel(jax.random.fold_in(splits[4], 71), 0)
    atom_slot = draw_atom_slot(jax.random.fold_in(splits[4], 71), 0)
    lag_offsets = draw_lag_offsets(jax.random.fold_in(splits[4], 71), 0)
    return {"velocities": velocities, "modes_panel": modes_panel, "atom_slot": atom_slot, "lag_offsets": lag_offsets}


def reference(velocities, modes_panel, atom_slot, lag_offsets):
    block_start = jnp.arange(NATOMS, dtype=jnp.int32) // ATOM_DEV * ATOM_DEV
    chosen = (block_start + atom_slot).astype(jnp.int32)
    per_atom = modes_panel.reshape(NATOMS, 3, M)
    panel_ordered = jnp.take(per_atom, chosen, axis=0).reshape(COORDS, M)
    projected = jnp.dot(velocities, panel_ordered, preferred_element_type=jnp.float32)
    energy = lax.optimization_barrier(jnp.sum(projected * projected, axis=1))
    normalized = (projected * lax.rsqrt(energy / M + 1e-06)[:, None]).astype(jnp.bfloat16)
    padded = jnp.concatenate([normalized, jnp.zeros((MAXLAG, M), jnp.bfloat16)], axis=0)

    def one_lag(offset):
        shifted = lax.dynamic_slice_in_dim(padded, offset.astype(jnp.int32), S, 0)
        product = lax.dot_general(normalized, shifted, (((0,), (0,)), ((), ())), preferred_element_type=jnp.float32)
        return product * lax.rsqrt((S - offset).astype(jnp.float32))
    return lax.map(one_lag, lag_offsets)
```

```python
import jax
import jax.numpy as jnp
from jax import lax
from jax.experimental import pallas as pl
from jax.experimental.pallas import tpu as pltpu
from jax.sharding import PartitionSpec as P

M = 4096
LAGS = 8
MAXLAG = 256
S = 1024
ATOMS = 2560
ROWS = 3 * ATOMS
WIDTH = 256
BLOCK = 128
CHUNKS = 4
UNIT = 16
epsilon = 1e-06

MESH = pl.DeviceIdType.MESH
VMEM = pltpu.VMEM
DMA = pltpu.SemaphoreType.DMA


def project_kernel(
    slot_ref, panel_hbm, v_hbm, row_out, col_out,
    panel, wide, ordered, v_buf, part, landed, energy_send, energy_land, block_t, block_n, moved,
    panel_sem, v_sem, rs_send, rs_recv, e_send, e_recv, c_send, c_recv, t_send, t_recv,
    b_send, b_recv, s_send, s_recv,
):
    r, c = lax.axis_index("row"), lax.axis_index("col")
    y, z = r // 2, r % 2
    chip, core = c // 2, c % 2
    zh, x = chip // 4, chip % 4

    piece = ROWS // CHUNKS
    panel_copies = []
    for i in range(CHUNKS):
        rows = pl.ds(i * piece, piece)
        panel_copies.append(
            pltpu.make_async_copy(panel_hbm.at[rows, :], panel.at[rows, :], panel_sem.at[i])
        )
        panel_copies[-1].start()
    quads = [lax.rem(y + d, 4) for d in (2, 1, 3, 0)]
    v_copies = []
    for i, q in enumerate(quads):
        rows = pl.ds(pl.multiple_of(q * 256, 256), 256)
        v_copies.append(pltpu.make_async_copy(v_hbm.at[rows, :], v_buf.at[i], v_sem.at[i]))
        v_copies[-1].start()

    barrier = pltpu.get_barrier_semaphore()
    for d in range(1, 8):
        pl.semaphore_signal(barrier, inc=1, device_id=(lax.rem(r + d, 8), c), device_id_type=MESH)
    for d in range(1, 16):
        pl.semaphore_signal(barrier, inc=1, device_id=(r, lax.rem(c + d, 16)), device_id_type=MESH)
    partner = (chip, 2 * r + core)
    moves = chip != r

    @pl.when(moves)
    def _():
        pl.semaphore_signal(barrier, inc=1, device_id=partner, device_id_type=MESH)

    for i in range(CHUNKS):
        panel_copies[i].wait()

        def widen(n, _, i=i):
            start = pl.multiple_of(i * piece + n * 64, 64)
            v = panel[pl.ds(start, 64), :].astype(jnp.float32)
            wide[0, pl.ds(8 + start, 64), :] = v[:, :128]
            wide[1, pl.ds(8 + start, 64), :] = v[:, 128:]
            return 0

        lax.fori_loop(0, piece // 64, widen, 0)
    sub = lax.broadcasted_iota(jnp.int32, (8, 128), 0)

    def take(g, _):
        base = [3 * slot_ref[g * UNIT + u] + 8 for u in range(UNIT)]
        for h in range(2):
            tiles = []
            for t in range(3 * UNIT // 8):
                tile = None
                for u in range(UNIT):
                    low = 3 * u - 8 * t
                    if low <= -3 or low >= 8:
                        continue
                    v = wide[h, pl.ds(base[u] - low, 8), :]
                    tile = v if tile is None else jnp.where(sub >= low, v, tile)
                tiles.append(tile)
            for t in range(0, len(tiles), 2):
                both = jnp.concatenate([tiles[t], tiles[t + 1]], axis=0).astype(jnp.bfloat16)
                at = pl.multiple_of(g * (3 * UNIT) + t * 8, 16)
                ordered[pl.ds(at, 16), h * 128 : (h + 1) * 128] = both
        return 0

    lax.fori_loop(0, ATOMS // UNIT, take, 0)

    pl.semaphore_wait(barrier, jnp.where(moves, 23, 22))

    rs_copies = []
    for i, q in enumerate(quads):
        v_copies[i].wait()
        part[i] = jnp.dot(v_buf[i], ordered[...], preferred_element_type=jnp.float32)
        for zz in range(2):
            k = 2 * i + zz
            if k == 7:
                continue
            to_z = lax.rem(z + 1 + zz, 2)
            rows = pl.ds(pl.multiple_of(to_z * BLOCK, BLOCK), BLOCK)
            copy = pltpu.make_async_remote_copy(
                src_ref=part.at[i, rows, :], dst_ref=landed.at[k],
                send_sem=rs_send.at[k], recv_sem=rs_recv.at[k],
                device_id=(2 * q + to_z, c), device_id_type=MESH,
            )
            copy.start()
            rs_copies.append(copy)
    mine = part[3, pl.ds(pl.multiple_of(z * BLOCK, BLOCK), BLOCK), :]
    for k in range(7):
        rs_copies[k].wait_recv()
        mine = mine + landed[k]

    turned = mine.T
    own = jnp.sum(turned * turned, axis=0, keepdims=True)
    energy_send[...] = jnp.broadcast_to(own, (8, BLOCK))
    e_copies = []
    for d in range(1, 16):
        copy = pltpu.make_async_remote_copy(
            src_ref=energy_send, dst_ref=energy_land.at[d - 1],
            send_sem=e_send.at[d - 1], recv_sem=e_recv.at[d - 1],
            device_id=(r, lax.rem(c + d, 16)), device_id_type=MESH,
        )
        copy.start()
        e_copies.append(copy)
    total = own
    for d in range(15):
        e_copies[d].wait_recv()
        total = total + energy_land[d, 0:1, :]
    scaled = turned * lax.rsqrt(total / M + epsilon)
    block_t[...] = scaled.astype(jnp.bfloat16)

    t_copy = pltpu.make_async_remote_copy(
        src_ref=block_t, dst_ref=moved, send_sem=t_send, recv_sem=t_recv,
        device_id=partner, device_id_type=MESH,
    )

    @pl.when(moves)
    def _():
        t_copy.start()

    block_n[...] = scaled.T.astype(jnp.bfloat16)
    own_rows = pl.ds(pl.multiple_of(r * BLOCK, BLOCK), BLOCK)
    c_copies = []
    for d in range(1, 8):
        copy = pltpu.make_async_remote_copy(
            src_ref=block_n, dst_ref=col_out.at[own_rows, :],
            send_sem=c_send.at[d - 1], recv_sem=c_recv.at[d - 1],
            device_id=(lax.rem(r + d, 8), c), device_id_type=MESH,
        )
        copy.start()
        c_copies.append(copy)
    col_out[own_rows, :] = block_n[...]

    @pl.when(moves)
    def _():
        t_copy.wait_recv()

    @pl.when(jnp.logical_not(moves))
    def _():
        moved[...] = block_t[...]

    def place(of_core, of_chip):
        return (
            pl.ds(pl.multiple_of(of_core * WIDTH, WIDTH), WIDTH),
            pl.ds(pl.multiple_of(of_chip * BLOCK, BLOCK), BLOCK),
        )

    here = place(core, chip)
    b_copies = []
    for d in range(1, 8):
        to_chip = lax.rem(zh + d // 4, 2) * 4 + lax.rem(x + d % 4, 4)
        copy = pltpu.make_async_remote_copy(
            src_ref=moved, dst_ref=row_out.at[here],
            send_sem=b_send.at[d - 1], recv_sem=b_recv.at[d - 1],
            device_id=(r, 2 * to_chip + core), device_id_type=MESH,
        )
        copy.start()
        b_copies.append(copy)
    row_out[here] = moved[...]
    other = (r, 2 * chip + 1 - core)
    s_copies = []
    for d in range(8):
        if d:
            b_copies[d - 1].wait_recv()
        from_chip = lax.rem(zh + d // 4, 2) * 4 + lax.rem(x + 4 - d % 4, 4)
        spot = place(core, from_chip)
        copy = pltpu.make_async_remote_copy(
            src_ref=row_out.at[spot] if d else moved, dst_ref=row_out.at[spot],
            send_sem=s_send.at[d], recv_sem=s_recv.at[d],
            device_id=other, device_id_type=MESH,
        )
        copy.start()
        s_copies.append(copy)
    for d in range(8):
        s_copies[d].wait_recv()
    for d in range(7):
        c_copies[d].wait_recv()

    for copy in (*rs_copies, *e_copies, *c_copies, *b_copies, *s_copies):
        copy.wait_send()

    @pl.when(moves)
    def _():
        t_copy.wait_send()


def project(velocities, modes_panel, atom_slot):
    return pl.pallas_call(
        project_kernel,
        out_shape=(
            jax.ShapeDtypeStruct((2 * WIDTH, S), jnp.bfloat16),
            jax.ShapeDtypeStruct((S, WIDTH), jnp.bfloat16),
        ),
        in_specs=[
            pl.BlockSpec(memory_space=pltpu.SMEM),
            pl.BlockSpec(memory_space=pl.ANY),
            pl.BlockSpec(memory_space=pl.ANY),
        ],
        out_specs=(pl.BlockSpec(memory_space=VMEM), pl.BlockSpec(memory_space=VMEM)),
        scratch_shapes=[
            VMEM((ROWS, WIDTH), jnp.bfloat16),
            VMEM((2, ROWS + 16, 128), jnp.float32),
            VMEM((ROWS, WIDTH), jnp.bfloat16),
            VMEM((4, 256, ROWS), jnp.bfloat16),
            VMEM((4, 256, WIDTH), jnp.float32),
            VMEM((7, BLOCK, WIDTH), jnp.float32),
            VMEM((8, BLOCK), jnp.float32),
            VMEM((15, 8, BLOCK), jnp.float32),
            VMEM((WIDTH, BLOCK), jnp.bfloat16),
            VMEM((BLOCK, WIDTH), jnp.bfloat16),
            VMEM((WIDTH, BLOCK), jnp.bfloat16),
            DMA((CHUNKS,)), DMA((4,)),
            DMA((7,)), DMA((7,)),
            DMA((15,)), DMA((15,)),
            DMA((7,)), DMA((7,)),
            DMA, DMA,
            DMA((7,)), DMA((7,)),
            DMA((8,)), DMA((8,)),
        ],
        compiler_params=pltpu.CompilerParams(
            collective_id=0, has_side_effects=True, vmem_limit_bytes=52 * 2**20
        ),
    )(atom_slot, modes_panel, velocities)


def correlate_kernel(lag_ref, rows_ref, cols_ref, out_ref, padded):
    step = pl.program_id(0)

    @pl.when(step == 0)
    def _():
        for h in range(2):
            padded[h, :S, :] = cols_ref[:, h * 128 : (h + 1) * 128].astype(jnp.float32)
            padded[h, S:, :] = jnp.zeros((MAXLAG, 128), jnp.float32)

    lag = lag_ref[step]
    shifted = jnp.concatenate(
        [padded[h, pl.ds(lag, S), :].astype(jnp.bfloat16) for h in range(2)], axis=1
    )
    product = jnp.dot(rows_ref[...], shifted, preferred_element_type=jnp.float32)
    count = jnp.broadcast_to((S - lag).astype(jnp.float32), (1, WIDTH))
    out_ref[0] = product * lax.rsqrt(count)


def correlate(row_modes, column_modes, lag_offsets):
    return pl.pallas_call(
        correlate_kernel,
        grid=(LAGS,),
        out_shape=jax.ShapeDtypeStruct((LAGS, 2 * WIDTH, WIDTH), jnp.float32),
        in_specs=[
            pl.BlockSpec(memory_space=pltpu.SMEM),
            pl.BlockSpec(memory_space=VMEM),
            pl.BlockSpec(memory_space=VMEM),
        ],
        out_specs=pl.BlockSpec((1, 2 * WIDTH, WIDTH), lambda i: (i, 0, 0)),
        scratch_shapes=[VMEM((2, S + MAXLAG, 128), jnp.float32)],
        compiler_params=pltpu.CompilerParams(vmem_limit_bytes=24 * 2**20),
    )(lag_offsets, row_modes, column_modes)


def local(velocities, modes_panel, atom_slot, lag_offsets):
    row_modes, column_modes = project(velocities, modes_panel, atom_slot)
    return correlate(row_modes, column_modes, lag_offsets)


def solution(mesh):
    return jax.shard_map(
        local,
        mesh=mesh,
        in_specs=(P(None, "row"), P("row", "col"), P("row"), P()),
        out_specs=P(None, "row", "col"),
        check_vma=False,
    )
```

```python
import jax
import jax.numpy as jnp
from jax import lax
from jax.experimental import pallas as pl
from jax.experimental.pallas import tpu as pltpu
from jax.sharding import PartitionSpec as P

M = 4096
LAGS = 8
MAXLAG = 256
S = 1024
ATOMS = 2560
ROWS = 3 * ATOMS
WIDTH = 256
BLOCK = 128
CHUNKS = 4
UNIT = 16
epsilon = 1e-06

MESH = pl.DeviceIdType.MESH
VMEM = pltpu.VMEM
DMA = pltpu.SemaphoreType.DMA


def project_kernel(
    slot_hbm, panel_hbm, v_hbm, row_out, col_out,
    slot_ref, panel, wide, ordered, v_buf, part, landed, energy_send, energy_land, block_t, block_n, moved,
    slot_sem, panel_sem, v_sem, rs_send, rs_recv, e_send, e_recv, c_send, c_recv, t_send, t_recv,
    b_send, b_recv, s_send, s_recv,
):
    r, c = lax.axis_index("row"), lax.axis_index("col")
    y, z = r // 2, r % 2
    chip, core = c // 2, c % 2
    zh, x = chip // 4, chip % 4

    slot_copy = pltpu.make_async_copy(slot_hbm, slot_ref, slot_sem)
    slot_copy.start()
    piece = ROWS // CHUNKS
    panel_copies = []
    for i in range(CHUNKS):
        rows = pl.ds(i * piece, piece)
        panel_copies.append(
            pltpu.make_async_copy(panel_hbm.at[rows, :], panel.at[rows, :], panel_sem.at[i])
        )
        panel_copies[-1].start()
    quads = [lax.rem(y + d, 4) for d in (2, 1, 3, 0)]
    v_copies = []
    for i, q in enumerate(quads):
        rows = pl.ds(pl.multiple_of(q * 256, 256), 256)
        v_copies.append(pltpu.make_async_copy(v_hbm.at[rows, :], v_buf.at[i], v_sem.at[i]))

    barrier = pltpu.get_barrier_semaphore()
    for d in range(1, 8):
        pl.semaphore_signal(barrier, inc=1, device_id=(lax.rem(r + d, 8), c), device_id_type=MESH)
    for d in range(1, 16):
        pl.semaphore_signal(barrier, inc=1, device_id=(r, lax.rem(c + d, 16)), device_id_type=MESH)
    partner = (chip, 2 * r + core)
    moves = chip != r

    @pl.when(moves)
    def _():
        pl.semaphore_signal(barrier, inc=1, device_id=partner, device_id_type=MESH)

    for i in range(CHUNKS):
        panel_copies[i].wait()
        if i == CHUNKS - 1:
            for copy in v_copies:
                copy.start()

        def widen(n, _, i=i):
            start = pl.multiple_of(i * piece + n * 64, 64)
            v = panel[pl.ds(start, 64), :].astype(jnp.float32)
            wide[0, pl.ds(8 + start, 64), :] = v[:, :128]
            wide[1, pl.ds(8 + start, 64), :] = v[:, 128:]
            return 0

        lax.fori_loop(0, piece // 64, widen, 0)
    slot_copy.wait()
    sub = lax.broadcasted_iota(jnp.int32, (8, 128), 0)

    def take(g, _):
        base = [3 * slot_ref[g * UNIT + u] + 8 for u in range(UNIT)]
        for h in range(2):
            tiles = []
            for t in range(3 * UNIT // 8):
                tile = None
                for u in range(UNIT):
                    low = 3 * u - 8 * t
                    if low <= -3 or low >= 8:
                        continue
                    v = wide[h, pl.ds(base[u] - low, 8), :]
                    tile = v if tile is None else jnp.where(sub >= low, v, tile)
                tiles.append(tile)
            for t in range(0, len(tiles), 2):
                both = jnp.concatenate([tiles[t], tiles[t + 1]], axis=0).astype(jnp.bfloat16)
                at = pl.multiple_of(g * (3 * UNIT) + t * 8, 16)
                ordered[pl.ds(at, 16), h * 128 : (h + 1) * 128] = both
        return 0

    lax.fori_loop(0, ATOMS // UNIT, take, 0)

    pl.semaphore_wait(barrier, jnp.where(moves, 23, 22))

    rs_copies = []
    for i, q in enumerate(quads):
        v_copies[i].wait()
        part[i] = jnp.dot(v_buf[i], ordered[...], preferred_element_type=jnp.float32)
        for zz in range(2):
            k = 2 * i + zz
            if k == 7:
                continue
            to_z = lax.rem(z + 1 + zz, 2)
            rows = pl.ds(pl.multiple_of(to_z * BLOCK, BLOCK), BLOCK)
            copy = pltpu.make_async_remote_copy(
                src_ref=part.at[i, rows, :], dst_ref=landed.at[k],
                send_sem=rs_send.at[k], recv_sem=rs_recv.at[k],
                device_id=(2 * q + to_z, c), device_id_type=MESH,
            )
            copy.start()
            rs_copies.append(copy)
    mine = part[3, pl.ds(pl.multiple_of(z * BLOCK, BLOCK), BLOCK), :]
    for k in range(7):
        rs_copies[k].wait_recv()
        mine = mine + landed[k]

    turned = mine.T
    own = jnp.sum(turned * turned, axis=0, keepdims=True)
    energy_send[...] = jnp.broadcast_to(own, (8, BLOCK))
    e_copies = []
    for d in range(1, 16):
        copy = pltpu.make_async_remote_copy(
            src_ref=energy_send, dst_ref=energy_land.at[d - 1],
            send_sem=e_send.at[d - 1], recv_sem=e_recv.at[d - 1],
            device_id=(r, lax.rem(c + d, 16)), device_id_type=MESH,
        )
        copy.start()
        e_copies.append(copy)
    total = own
    for d in range(15):
        e_copies[d].wait_recv()
        total = total + energy_land[d, 0:1, :]
    scaled = turned * lax.rsqrt(total / M + epsilon)
    block_t[...] = scaled.astype(jnp.bfloat16)

    t_copy = pltpu.make_async_remote_copy(
        src_ref=block_t, dst_ref=moved, send_sem=t_send, recv_sem=t_recv,
        device_id=partner, device_id_type=MESH,
    )

    @pl.when(moves)
    def _():
        t_copy.start()

    block_n[...] = scaled.T.astype(jnp.bfloat16)

    def rows_of(of_row):
        return pl.ds(pl.multiple_of(of_row * BLOCK, BLOCK), BLOCK)

    def place(of_chip):
        return (
            pl.ds(pl.multiple_of(core * WIDTH, WIDTH), WIDTH),
            pl.ds(pl.multiple_of(of_chip * BLOCK, BLOCK), BLOCK),
        )

    def to_row(k, src, rows, device):
        copy = pltpu.make_async_remote_copy(
            src_ref=src, dst_ref=col_out.at[rows, :],
            send_sem=c_send.at[k], recv_sem=c_recv.at[k],
            device_id=(device, c), device_id_type=MESH,
        )
        copy.start()
        return copy

    def to_col(k, src, spot, chip_to):
        copy = pltpu.make_async_remote_copy(
            src_ref=src, dst_ref=row_out.at[spot],
            send_sem=b_send.at[k], recv_sem=b_recv.at[k],
            device_id=(r, 2 * chip_to + core), device_id_type=MESH,
        )
        copy.start()
        return copy

    def to_sibling(k, src, spot):
        copy = pltpu.make_async_remote_copy(
            src_ref=src, dst_ref=row_out.at[spot],
            send_sem=s_send.at[k], recv_sem=s_recv.at[k],
            device_id=(r, 2 * chip + 1 - core), device_id_type=MESH,
        )
        copy.start()
        return copy

    c_copies = [to_row(0, block_n, rows_of(r), 2 * y + 1 - z)]
    col_out[rows_of(r), :] = block_n[...]

    @pl.when(moves)
    def _():
        t_copy.wait_recv()

    @pl.when(jnp.logical_not(moves))
    def _():
        moved[...] = block_t[...]

    far = 4 * (1 - zh)
    near = 4 * zh
    b_copies = [to_col(0, moved, place(chip), far + x)]
    for d in (2, 1, 3):
        b_copies.append(to_col(d, moved, place(chip), near + lax.rem(x + d, 4)))
    for d in (2, 1, 3):
        c_copies.append(to_row(d, block_n, rows_of(r), 2 * lax.rem(y + d, 4) + z))
    s_copies = [to_sibling(0, moved, place(chip))]
    row_out[place(chip)] = moved[...]
    b_copies[0].wait_recv()
    other = place(far + x)
    for d in (2, 1, 3):
        b_copies.append(to_col(3 + d, row_out.at[other], other, near + lax.rem(x + d, 4)))
    c_copies[0].wait_recv()
    beside = rows_of(2 * y + 1 - z)
    for d in (2, 1, 3):
        c_copies.append(to_row(3 + d, col_out.at[beside, :], beside, 2 * lax.rem(y + d, 4) + z))
    s_copies.append(to_sibling(1, row_out.at[other], other))
    for n, side in enumerate((near, far)):
        for m, d in enumerate((2, 1, 3)):
            b_copies[1 + 3 * n + m].wait_recv()
            spot = place(side + lax.rem(x + 4 - d, 4))
            s_copies.append(to_sibling(2 + 3 * n + m, row_out.at[spot], spot))
    for copy in (*s_copies, *c_copies[1:]):
        copy.wait_recv()

    for copy in (*rs_copies, *e_copies, *c_copies, *b_copies, *s_copies):
        copy.wait_send()

    @pl.when(moves)
    def _():
        t_copy.wait_send()


def project(velocities, modes_panel, atom_slot):
    return pl.pallas_call(
        project_kernel,
        out_shape=(
            jax.ShapeDtypeStruct((2 * WIDTH, S), jnp.bfloat16),
            jax.ShapeDtypeStruct((S, WIDTH), jnp.bfloat16),
        ),
        in_specs=[
            pl.BlockSpec(memory_space=pltpu.HBM),
            pl.BlockSpec(memory_space=pltpu.HBM),
            pl.BlockSpec(memory_space=pltpu.HBM),
        ],
        out_specs=(pl.BlockSpec(memory_space=VMEM), pl.BlockSpec(memory_space=VMEM)),
        scratch_shapes=[
            pltpu.SMEM((ATOMS,), jnp.int32),
            VMEM((ROWS, WIDTH), jnp.bfloat16),
            VMEM((2, ROWS + 16, 128), jnp.float32),
            VMEM((ROWS, WIDTH), jnp.bfloat16),
            VMEM((4, 256, ROWS), jnp.bfloat16),
            VMEM((4, 256, WIDTH), jnp.float32),
            VMEM((7, BLOCK, WIDTH), jnp.float32),
            VMEM((8, BLOCK), jnp.float32),
            VMEM((15, 8, BLOCK), jnp.float32),
            VMEM((WIDTH, BLOCK), jnp.bfloat16),
            VMEM((BLOCK, WIDTH), jnp.bfloat16),
            VMEM((WIDTH, BLOCK), jnp.bfloat16),
            DMA, DMA((CHUNKS,)), DMA((4,)),
            DMA((7,)), DMA((7,)),
            DMA((15,)), DMA((15,)),
            DMA((7,)), DMA((7,)),
            DMA, DMA,
            DMA((7,)), DMA((7,)),
            DMA((8,)), DMA((8,)),
        ],
        compiler_params=pltpu.CompilerParams(
            collective_id=0, has_side_effects=True, vmem_limit_bytes=52 * 2**20
        ),
    )(atom_slot, modes_panel, velocities)


def correlate_kernel(lag_ref, rows_ref, cols_ref, out_hbm, padded, shifted, held, out_sem):
    for h in range(2):
        padded[h, :S, :] = cols_ref[:, h * 128 : (h + 1) * 128].astype(jnp.float32)
        padded[h, S:, :] = jnp.zeros((MAXLAG, 128), jnp.float32)
    copies = []
    for i in range(LAGS):
        lag = lag_ref[i]
        for h in range(2):
            cut = padded[h, pl.ds(lag, S), :].astype(jnp.bfloat16)
            shifted[i % 2, :, h * 128 : (h + 1) * 128] = cut
        factor = lax.rsqrt(jnp.broadcast_to((S - lag).astype(jnp.float32), (1, WIDTH)))
        for p in range(2):
            rows = pl.ds(p * WIDTH, WIDTH)
            product = jnp.dot(
                rows_ref[rows, :], shifted[i % 2], preferred_element_type=jnp.float32
            )
            held[i, rows, :] = product * factor
        copies.append(pltpu.make_async_copy(held.at[i], out_hbm.at[i], out_sem.at[i]))
        copies[-1].start()
    for copy in copies:
        copy.wait()


def correlate(row_modes, column_modes, lag_offsets):
    return pl.pallas_call(
        correlate_kernel,
        out_shape=jax.ShapeDtypeStruct((LAGS, 2 * WIDTH, WIDTH), jnp.float32),
        in_specs=[
            pl.BlockSpec(memory_space=pltpu.SMEM),
            pl.BlockSpec(memory_space=VMEM),
            pl.BlockSpec(memory_space=VMEM),
        ],
        out_specs=pl.BlockSpec(memory_space=pl.ANY),
        scratch_shapes=[
            VMEM((2, S + MAXLAG, 128), jnp.float32),
            VMEM((2, S, WIDTH), jnp.bfloat16),
            VMEM((LAGS, 2 * WIDTH, WIDTH), jnp.float32),
            DMA((LAGS,)),
        ],
        compiler_params=pltpu.CompilerParams(vmem_limit_bytes=24 * 2**20),
    )(lag_offsets, row_modes, column_modes)


def local(velocities, modes_panel, atom_slot, lag_offsets):
    row_modes, column_modes = project(velocities, modes_panel, atom_slot)
    return correlate(row_modes, column_modes, lag_offsets)


def solution(mesh):
    return jax.shard_map(
        local,
        mesh=mesh,
        in_specs=(P(None, "row"), P("row", "col"), P("row"), P()),
        out_specs=P(None, "row", "col"),
        check_vma=False,
    )
```

```python
import jax
import jax.numpy as jnp
from jax import lax
from jax.experimental import pallas as pl
from jax.experimental.pallas import tpu as pltpu
from jax.sharding import PartitionSpec as P

M = 4096
LAGS = 8
MAXLAG = 256
S = 1024
ATOMS = 2560
ROWS = 3 * ATOMS
WIDTH = 256
BLOCK = 128
CHUNKS = 4
UNIT = 16
TINY = 1e-30
epsilon = 1e-06

MESH = pl.DeviceIdType.MESH
VMEM = pltpu.VMEM
DMA = pltpu.SemaphoreType.DMA


def project_kernel(
    slot_hbm, panel_hbm, v_hbm, row_out, col_out,
    slot_ref, panel, wide, ordered, v_buf, sent, landed, energy_send, energy_land, block_t, block_n, moved,
    slot_sem, panel_sem, v_sem, rs_send, rs_recv, e_send, e_recv, c_send, c_recv, t_send, t_recv,
    b_send, b_recv, s_send, s_recv,
):
    r, c = lax.axis_index("row"), lax.axis_index("col")
    y, z = r // 2, r % 2
    chip, core = c // 2, c % 2
    zh, x = chip // 4, chip % 4

    slot_copy = pltpu.make_async_copy(slot_hbm, slot_ref, slot_sem)
    slot_copy.start()
    piece = ROWS // CHUNKS
    panel_copies = []
    for i in range(CHUNKS):
        rows = pl.ds(i * piece, piece)
        panel_copies.append(
            pltpu.make_async_copy(panel_hbm.at[rows, :], panel.at[rows, :], panel_sem.at[i])
        )
        panel_copies[-1].start()
    quads = [lax.rem(y + d, 4) for d in (2, 1, 3, 0)]
    v_copies = []
    for i, q in enumerate(quads):
        rows = pl.ds(pl.multiple_of(q * 256, 256), 256)
        v_copies.append(pltpu.make_async_copy(v_hbm.at[rows, :], v_buf.at[i], v_sem.at[i]))

    barrier = pltpu.get_barrier_semaphore()
    for d in range(1, 8):
        pl.semaphore_signal(barrier, inc=1, device_id=(lax.rem(r + d, 8), c), device_id_type=MESH)
    for d in range(1, 16):
        pl.semaphore_signal(barrier, inc=1, device_id=(r, lax.rem(c + d, 16)), device_id_type=MESH)
    partner = (chip, 2 * r + core)
    moves = chip != r

    @pl.when(moves)
    def _():
        pl.semaphore_signal(barrier, inc=1, device_id=partner, device_id_type=MESH)

    for i in range(CHUNKS):
        panel_copies[i].wait()
        if i == CHUNKS - 1:
            for copy in v_copies:
                copy.start()

        def widen(n, _, i=i):
            start = pl.multiple_of(i * piece + n * 64, 64)
            v = panel[pl.ds(start, 64), :].astype(jnp.float32)
            wide[0, pl.ds(8 + start, 64), :] = v[:, :128]
            wide[1, pl.ds(8 + start, 64), :] = v[:, 128:]
            return 0

        lax.fori_loop(0, piece // 64, widen, 0)
    slot_copy.wait()
    sub = lax.broadcasted_iota(jnp.int32, (8, 128), 0)

    def take(g, _):
        base = [3 * slot_ref[g * UNIT + u] + 8 for u in range(UNIT)]
        for h in range(2):
            tiles = []
            for t in range(3 * UNIT // 8):
                tile = None
                for u in range(UNIT):
                    low = 3 * u - 8 * t
                    if low <= -3 or low >= 8:
                        continue
                    v = wide[h, pl.ds(base[u] - low, 8), :]
                    tile = v if tile is None else jnp.where(sub >= low, v, tile)
                tiles.append(tile)
            for t in range(0, len(tiles), 2):
                both = jnp.concatenate([tiles[t], tiles[t + 1]], axis=0).astype(jnp.bfloat16)
                at = pl.multiple_of(g * (3 * UNIT) + t * 8, 16)
                ordered[pl.ds(at, 16), h * 128 : (h + 1) * 128] = both
        return 0

    lax.fori_loop(0, ATOMS // UNIT, take, 0)

    pl.semaphore_wait(barrier, jnp.where(moves, 23, 22))

    rs_copies = []
    mine = None
    for i, q in enumerate(quads):
        v_copies[i].wait()
        part = jnp.dot(v_buf[i], ordered[...], preferred_element_type=jnp.float32)
        part = part.T
        top = jnp.max(jnp.abs(part), axis=0, keepdims=True)
        power = jnp.ceil(jnp.log2(jnp.maximum(top, TINY)))
        coded = jnp.clip(jnp.round(part * jnp.exp2(15.0 - power)), -32767.0, 32767.0)
        coded = coded.astype(jnp.int32).astype(jnp.int16)
        powers = jnp.broadcast_to(power, (16, 2 * BLOCK)).astype(jnp.int32).astype(jnp.int16)
        for zz in range(2):
            half = slice(zz * BLOCK, (zz + 1) * BLOCK)
            sent[i, zz, :WIDTH, :] = coded[:, half]
            sent[i, zz, WIDTH:, :] = powers[:, half]
        if i == 3:
            mine = jnp.where(z == 0, part[:, :BLOCK], part[:, BLOCK:])
        for zz in range(2):
            k = 2 * i + zz
            if k == 7:
                continue
            to_z = lax.rem(z + 1 + zz, 2)
            copy = pltpu.make_async_remote_copy(
                src_ref=sent.at[i, to_z], dst_ref=landed.at[k],
                send_sem=rs_send.at[k], recv_sem=rs_recv.at[k],
                device_id=(2 * q + to_z, c), device_id_type=MESH,
            )
            copy.start()
            rs_copies.append(copy)
    turned = mine
    for k in range(7):
        rs_copies[k].wait_recv()
        power = landed[k, WIDTH:, :].astype(jnp.int32).astype(jnp.float32)[0:1, :]
        value = landed[k, :WIDTH, :].astype(jnp.int32).astype(jnp.float32)
        turned = turned + value * jnp.exp2(power - 15.0)

    own = jnp.sum(turned * turned, axis=0, keepdims=True)
    energy_send[...] = jnp.broadcast_to(own, (8, BLOCK))
    e_copies = []
    for d in range(1, 16):
        copy = pltpu.make_async_remote_copy(
            src_ref=energy_send, dst_ref=energy_land.at[d - 1],
            send_sem=e_send.at[d - 1], recv_sem=e_recv.at[d - 1],
            device_id=(r, lax.rem(c + d, 16)), device_id_type=MESH,
        )
        copy.start()
        e_copies.append(copy)
    total = own
    for d in range(15):
        e_copies[d].wait_recv()
        total = total + energy_land[d, 0:1, :]
    scaled = turned * lax.rsqrt(total / M + epsilon)
    block_t[...] = scaled.astype(jnp.bfloat16)

    t_copy = pltpu.make_async_remote_copy(
        src_ref=block_t, dst_ref=moved, send_sem=t_send, recv_sem=t_recv,
        device_id=partner, device_id_type=MESH,
    )

    @pl.when(moves)
    def _():
        t_copy.start()

    block_n[...] = scaled.T.astype(jnp.bfloat16)

    def rows_of(of_row):
        return pl.ds(pl.multiple_of(of_row * BLOCK, BLOCK), BLOCK)

    def place(of_chip):
        return (
            pl.ds(pl.multiple_of(core * WIDTH, WIDTH), WIDTH),
            pl.ds(pl.multiple_of(of_chip * BLOCK, BLOCK), BLOCK),
        )

    def to_row(k, src, rows, device):
        copy = pltpu.make_async_remote_copy(
            src_ref=src, dst_ref=col_out.at[rows, :],
            send_sem=c_send.at[k], recv_sem=c_recv.at[k],
            device_id=(device, c), device_id_type=MESH,
        )
        copy.start()
        return copy

    def to_col(k, src, spot, chip_to):
        copy = pltpu.make_async_remote_copy(
            src_ref=src, dst_ref=row_out.at[spot],
            send_sem=b_send.at[k], recv_sem=b_recv.at[k],
            device_id=(r, 2 * chip_to + core), device_id_type=MESH,
        )
        copy.start()
        return copy

    def to_sibling(k, src, spot):
        copy = pltpu.make_async_remote_copy(
            src_ref=src, dst_ref=row_out.at[spot],
            send_sem=s_send.at[k], recv_sem=s_recv.at[k],
            device_id=(r, 2 * chip + 1 - core), device_id_type=MESH,
        )
        copy.start()
        return copy

    c_copies = [to_row(0, block_n, rows_of(r), 2 * y + 1 - z)]
    col_out[rows_of(r), :] = block_n[...]

    @pl.when(moves)
    def _():
        t_copy.wait_recv()

    @pl.when(jnp.logical_not(moves))
    def _():
        moved[...] = block_t[...]

    far = 4 * (1 - zh)
    near = 4 * zh
    b_copies = [to_col(0, moved, place(chip), far + x)]
    for d in (2, 1, 3):
        b_copies.append(to_col(d, moved, place(chip), near + lax.rem(x + d, 4)))
    for d in (2, 1, 3):
        c_copies.append(to_row(d, block_n, rows_of(r), 2 * lax.rem(y + d, 4) + z))
    s_copies = [to_sibling(0, moved, place(chip))]
    row_out[place(chip)] = moved[...]
    b_copies[0].wait_recv()
    other = place(far + x)
    for d in (2, 1, 3):
        b_copies.append(to_col(3 + d, row_out.at[other], other, near + lax.rem(x + d, 4)))
    c_copies[0].wait_recv()
    beside = rows_of(2 * y + 1 - z)
    for d in (2, 1, 3):
        c_copies.append(to_row(3 + d, col_out.at[beside, :], beside, 2 * lax.rem(y + d, 4) + z))
    s_copies.append(to_sibling(1, row_out.at[other], other))
    for n, side in enumerate((near, far)):
        for m, d in enumerate((2, 1, 3)):
            b_copies[1 + 3 * n + m].wait_recv()
            spot = place(side + lax.rem(x + 4 - d, 4))
            s_copies.append(to_sibling(2 + 3 * n + m, row_out.at[spot], spot))
    for copy in (*s_copies, *c_copies[1:]):
        copy.wait_recv()

    for copy in (*rs_copies, *e_copies, *c_copies, *b_copies, *s_copies):
        copy.wait_send()

    @pl.when(moves)
    def _():
        t_copy.wait_send()


def project(velocities, modes_panel, atom_slot):
    return pl.pallas_call(
        project_kernel,
        out_shape=(
            jax.ShapeDtypeStruct((2 * WIDTH, S), jnp.bfloat16),
            jax.ShapeDtypeStruct((S, WIDTH), jnp.bfloat16),
        ),
        in_specs=[
            pl.BlockSpec(memory_space=pltpu.HBM),
            pl.BlockSpec(memory_space=pltpu.HBM),
            pl.BlockSpec(memory_space=pltpu.HBM),
        ],
        out_specs=(pl.BlockSpec(memory_space=VMEM), pl.BlockSpec(memory_space=VMEM)),
        scratch_shapes=[
            pltpu.SMEM((ATOMS,), jnp.int32),
            VMEM((ROWS, WIDTH), jnp.bfloat16),
            VMEM((2, ROWS + 16, 128), jnp.float32),
            VMEM((ROWS, WIDTH), jnp.bfloat16),
            VMEM((4, 256, ROWS), jnp.bfloat16),
            VMEM((4, 2, WIDTH + 16, BLOCK), jnp.int16),
            VMEM((7, WIDTH + 16, BLOCK), jnp.int16),
            VMEM((8, BLOCK), jnp.float32),
            VMEM((15, 8, BLOCK), jnp.float32),
            VMEM((WIDTH, BLOCK), jnp.bfloat16),
            VMEM((BLOCK, WIDTH), jnp.bfloat16),
            VMEM((WIDTH, BLOCK), jnp.bfloat16),
            DMA, DMA((CHUNKS,)), DMA((4,)),
            DMA((7,)), DMA((7,)),
            DMA((15,)), DMA((15,)),
            DMA((7,)), DMA((7,)),
            DMA, DMA,
            DMA((7,)), DMA((7,)),
            DMA((8,)), DMA((8,)),
        ],
        compiler_params=pltpu.CompilerParams(
            collective_id=0, has_side_effects=True, vmem_limit_bytes=52 * 2**20
        ),
    )(atom_slot, modes_panel, velocities)


def correlate_kernel(lag_ref, rows_ref, cols_ref, out_hbm, padded, shifted, held, out_sem):
    for h in range(2):
        padded[h, :S, :] = cols_ref[:, h * 128 : (h + 1) * 128].astype(jnp.float32)
        padded[h, S:, :] = jnp.zeros((MAXLAG, 128), jnp.float32)
    copies = []
    for i in range(LAGS):
        lag = lag_ref[i]
        for h in range(2):
            cut = padded[h, pl.ds(lag, S), :].astype(jnp.bfloat16)
            shifted[i % 2, :, h * 128 : (h + 1) * 128] = cut
        factor = lax.rsqrt(jnp.broadcast_to((S - lag).astype(jnp.float32), (1, WIDTH)))
        for p in range(2):
            rows = pl.ds(p * WIDTH, WIDTH)
            product = jnp.dot(
                rows_ref[rows, :], shifted[i % 2], preferred_element_type=jnp.float32
            )
            held[i, rows, :] = product * factor
        copies.append(pltpu.make_async_copy(held.at[i], out_hbm.at[i], out_sem.at[i]))
        copies[-1].start()
    for copy in copies:
        copy.wait()


def correlate(row_modes, column_modes, lag_offsets):
    return pl.pallas_call(
        correlate_kernel,
        out_shape=jax.ShapeDtypeStruct((LAGS, 2 * WIDTH, WIDTH), jnp.float32),
        in_specs=[
            pl.BlockSpec(memory_space=pltpu.SMEM),
            pl.BlockSpec(memory_space=VMEM),
            pl.BlockSpec(memory_space=VMEM),
        ],
        out_specs=pl.BlockSpec(memory_space=pl.ANY),
        scratch_shapes=[
            VMEM((2, S + MAXLAG, 128), jnp.float32),
            VMEM((2, S, WIDTH), jnp.bfloat16),
            VMEM((LAGS, 2 * WIDTH, WIDTH), jnp.float32),
            DMA((LAGS,)),
        ],
        compiler_params=pltpu.CompilerParams(vmem_limit_bytes=24 * 2**20),
    )(lag_offsets, row_modes, column_modes)


def local(velocities, modes_panel, atom_slot, lag_offsets):
    row_modes, column_modes = project(velocities, modes_panel, atom_slot)
    return correlate(row_modes, column_modes, lag_offsets)


def solution(mesh):
    return jax.shard_map(
        local,
        mesh=mesh,
        in_specs=(P(None, "row"), P("row", "col"), P("row"), P()),
        out_specs=P(None, "row", "col"),
        check_vma=False,
    )
```

```python
import jax
import jax.numpy as jnp
from jax import lax
from jax.experimental import pallas as pl
from jax.experimental.pallas import tpu as pltpu
from jax.sharding import PartitionSpec as P

M = 4096
LAGS = 8
MAXLAG = 256
S = 1024
ATOMS = 2560
ROWS = 3 * ATOMS
WIDTH = 256
BLOCK = 128
CHUNKS = 4
UNIT = 16
TINY = 1e-30
epsilon = 1e-06

MESH = pl.DeviceIdType.MESH
VMEM = pltpu.VMEM
DMA = pltpu.SemaphoreType.DMA


def code(values):
    top = jnp.max(jnp.abs(values), axis=0, keepdims=True)
    power = jnp.ceil(jnp.log2(jnp.maximum(top, TINY)))
    coded = jnp.clip(jnp.round(values * jnp.exp2(15.0 - power)), -32767.0, 32767.0)
    powers = jnp.broadcast_to(power, (16, values.shape[1]))
    return coded.astype(jnp.int32).astype(jnp.int16), powers.astype(jnp.int32).astype(jnp.int16)


def decode(ref):
    power = ref[WIDTH:, :].astype(jnp.int32).astype(jnp.float32)[0:1, :]
    return ref[:WIDTH, :].astype(jnp.int32).astype(jnp.float32) * jnp.exp2(power - 15.0)


def project_kernel(
    slot_hbm, panel_hbm, v_hbm, row_out, col_out,
    slot_ref, panel, wide, ordered, v_buf, sent, landed, energy_send, energy_land, there_land, t_sent, t_land, block_n, moved,
    slot_sem, panel_sem, v_sem, rs_send, rs_recv, e_send, e_recv, there_send, there_recv, c_send, c_recv, t_send, t_recv,
    b_send, b_recv, s_send, s_recv,
):
    r, c = lax.axis_index("row"), lax.axis_index("col")
    y, z = r // 2, r % 2
    chip, core = c // 2, c % 2
    zh, x = chip // 4, chip % 4

    slot_copy = pltpu.make_async_copy(slot_hbm, slot_ref, slot_sem)
    slot_copy.start()
    piece = ROWS // CHUNKS
    panel_copies = []
    for i in range(CHUNKS):
        rows = pl.ds(i * piece, piece)
        panel_copies.append(
            pltpu.make_async_copy(panel_hbm.at[rows, :], panel.at[rows, :], panel_sem.at[i])
        )
        panel_copies[-1].start()
    quads = [lax.rem(y + d, 4) for d in (2, 1, 3, 0)]
    v_copies = []
    for i, q in enumerate(quads):
        rows = pl.ds(pl.multiple_of(q * 256, 256), 256)
        v_copies.append(pltpu.make_async_copy(v_hbm.at[rows, :], v_buf.at[i], v_sem.at[i]))

    barrier = pltpu.get_barrier_semaphore()
    for d in range(1, 8):
        pl.semaphore_signal(barrier, inc=1, device_id=(lax.rem(r + d, 8), c), device_id_type=MESH)
    for d in range(1, 16):
        pl.semaphore_signal(barrier, inc=1, device_id=(r, lax.rem(c + d, 16)), device_id_type=MESH)
    partner = (chip, 2 * r + core)
    moves = chip != r

    @pl.when(moves)
    def _():
        for k in range(16):
            pl.semaphore_signal(barrier, inc=1, device_id=(chip, k), device_id_type=MESH)

    for i in range(CHUNKS):
        panel_copies[i].wait()
        if i == CHUNKS - 1:
            for copy in v_copies:
                copy.start()

        def widen(n, _, i=i):
            start = pl.multiple_of(i * piece + n * 64, 64)
            v = panel[pl.ds(start, 64), :].astype(jnp.float32)
            wide[0, pl.ds(8 + start, 64), :] = v[:, :128]
            wide[1, pl.ds(8 + start, 64), :] = v[:, 128:]
            return 0

        lax.fori_loop(0, piece // 64, widen, 0)
    slot_copy.wait()
    sub = lax.broadcasted_iota(jnp.int32, (8, 128), 0)

    def take(g, _):
        base = [3 * slot_ref[g * UNIT + u] + 8 for u in range(UNIT)]
        for h in range(2):
            tiles = []
            for t in range(3 * UNIT // 8):
                tile = None
                for u in range(UNIT):
                    low = 3 * u - 8 * t
                    if low <= -3 or low >= 8:
                        continue
                    v = wide[h, pl.ds(base[u] - low, 8), :]
                    tile = v if tile is None else jnp.where(sub >= low, v, tile)
                tiles.append(tile)
            for t in range(0, len(tiles), 2):
                both = jnp.concatenate([tiles[t], tiles[t + 1]], axis=0).astype(jnp.bfloat16)
                at = pl.multiple_of(g * (3 * UNIT) + t * 8, 16)
                ordered[pl.ds(at, 16), h * 128 : (h + 1) * 128] = both
        return 0

    lax.fori_loop(0, ATOMS // UNIT, take, 0)

    pl.semaphore_wait(barrier, 36)

    rs_copies = []
    mine = None
    for i, q in enumerate(quads):
        v_copies[i].wait()
        part = jnp.dot(v_buf[i], ordered[...], preferred_element_type=jnp.float32)
        part = part.T
        coded, powers = code(part)
        for zz in range(2):
            half = slice(zz * BLOCK, (zz + 1) * BLOCK)
            sent[i, zz, :WIDTH, :] = coded[:, half]
            sent[i, zz, WIDTH:, :] = powers[:, half]
        if i == 3:
            mine = jnp.where(z == 0, part[:, :BLOCK], part[:, BLOCK:])
        for zz in range(2):
            k = 2 * i + zz
            if k == 7:
                continue
            to_z = lax.rem(z + 1 + zz, 2)
            copy = pltpu.make_async_remote_copy(
                src_ref=sent.at[i, to_z], dst_ref=landed.at[k],
                send_sem=rs_send.at[k], recv_sem=rs_recv.at[k],
                device_id=(2 * q + to_z, c), device_id_type=MESH,
            )
            copy.start()
            rs_copies.append(copy)
    turned = mine
    for k in range(7):
        rs_copies[k].wait_recv()
        turned = turned + decode(landed.at[k])

    t_sent[:WIDTH, :], t_sent[WIDTH:, :] = code(turned)
    t_copy = pltpu.make_async_remote_copy(
        src_ref=t_sent, dst_ref=t_land, send_sem=t_send, recv_sem=t_recv,
        device_id=partner, device_id_type=MESH,
    )

    @pl.when(moves)
    def _():
        t_copy.start()

    own = jnp.sum(turned * turned, axis=0, keepdims=True)
    energy_send[...] = jnp.broadcast_to(own, (8, BLOCK))
    e_copies = []
    for d in range(1, 8):
        for k in range(2):
            n = 2 * (d - 1) + k
            copy = pltpu.make_async_remote_copy(
                src_ref=energy_send, dst_ref=there_land.at[c],
                send_sem=there_send.at[n], recv_sem=there_recv.at[c],
                device_id=(lax.rem(r + d, 8), 2 * r + k), device_id_type=MESH,
            )
            copy.start()
            e_copies.append(copy)
    own_copies = []
    for d in range(1, 16):
        copy = pltpu.make_async_remote_copy(
            src_ref=energy_send, dst_ref=energy_land.at[d - 1],
            send_sem=e_send.at[d - 1], recv_sem=e_recv.at[d - 1],
            device_id=(r, lax.rem(c + d, 16)), device_id_type=MESH,
        )
        copy.start()
        own_copies.append(copy)
    e_copies += own_copies
    total = own
    for d in range(15):
        own_copies[d].wait_recv()
        total = total + energy_land[d, 0:1, :]
    scaled = turned * lax.rsqrt(total / M + epsilon)
    block_n[...] = scaled.T.astype(jnp.bfloat16)

    def rows_of(of_row):
        return pl.ds(pl.multiple_of(of_row * BLOCK, BLOCK), BLOCK)

    def place(of_chip):
        return (
            pl.ds(pl.multiple_of(core * WIDTH, WIDTH), WIDTH),
            pl.ds(pl.multiple_of(of_chip * BLOCK, BLOCK), BLOCK),
        )

    def to_row(k, src, rows, device):
        copy = pltpu.make_async_remote_copy(
            src_ref=src, dst_ref=col_out.at[rows, :],
            send_sem=c_send.at[k], recv_sem=c_recv.at[k],
            device_id=(device, c), device_id_type=MESH,
        )
        copy.start()
        return copy

    def to_col(k, src, spot, chip_to):
        copy = pltpu.make_async_remote_copy(
            src_ref=src, dst_ref=row_out.at[spot],
            send_sem=b_send.at[k], recv_sem=b_recv.at[k],
            device_id=(r, 2 * chip_to + core), device_id_type=MESH,
        )
        copy.start()
        return copy

    def to_sibling(k, src, spot):
        copy = pltpu.make_async_remote_copy(
            src_ref=src, dst_ref=row_out.at[spot],
            send_sem=s_send.at[k], recv_sem=s_recv.at[k],
            device_id=(r, 2 * chip + 1 - core), device_id_type=MESH,
        )
        copy.start()
        return copy

    c_copies = [to_row(0, block_n, rows_of(r), 2 * y + 1 - z)]
    col_out[rows_of(r), :] = block_n[...]

    @pl.when(moves)
    def _():
        energy = jnp.zeros((1, BLOCK), jnp.float32)
        for k in range(16):
            pltpu.make_async_remote_copy(
                src_ref=energy_send, dst_ref=there_land.at[k],
                send_sem=there_send.at[0], recv_sem=there_recv.at[k],
                device_id=partner, device_id_type=MESH,
            ).wait_recv()
            energy = energy + there_land[k, 0:1, :]
        t_copy.wait_recv()
        moved[...] = (decode(t_land) * lax.rsqrt(energy / M + epsilon)).astype(jnp.bfloat16)

    @pl.when(jnp.logical_not(moves))
    def _():
        moved[...] = scaled.astype(jnp.bfloat16)

    far = 4 * (1 - zh)
    near = 4 * zh
    b_copies = [to_col(0, moved, place(chip), far + x)]
    for d in (2, 1, 3):
        b_copies.append(to_col(d, moved, place(chip), near + lax.rem(x + d, 4)))
    for d in (2, 1, 3):
        c_copies.append(to_row(d, block_n, rows_of(r), 2 * lax.rem(y + d, 4) + z))
    s_copies = [to_sibling(0, moved, place(chip))]
    row_out[place(chip)] = moved[...]
    b_copies[0].wait_recv()
    other = place(far + x)
    for d in (2, 1, 3):
        b_copies.append(to_col(3 + d, row_out.at[other], other, near + lax.rem(x + d, 4)))
    c_copies[0].wait_recv()
    beside = rows_of(2 * y + 1 - z)
    for d in (2, 1, 3):
        c_copies.append(to_row(3 + d, col_out.at[beside, :], beside, 2 * lax.rem(y + d, 4) + z))
    s_copies.append(to_sibling(1, row_out.at[other], other))
    for n, side in enumerate((near, far)):
        for m, d in enumerate((2, 1, 3)):
            b_copies[1 + 3 * n + m].wait_recv()
            spot = place(side + lax.rem(x + 4 - d, 4))
            s_copies.append(to_sibling(2 + 3 * n + m, row_out.at[spot], spot))
    for copy in (*s_copies, *c_copies[1:]):
        copy.wait_recv()

    for copy in (*rs_copies, *e_copies, *c_copies, *b_copies, *s_copies):
        copy.wait_send()

    @pl.when(moves)
    def _():
        t_copy.wait_send()


def project(velocities, modes_panel, atom_slot):
    return pl.pallas_call(
        project_kernel,
        out_shape=(
            jax.ShapeDtypeStruct((2 * WIDTH, S), jnp.bfloat16),
            jax.ShapeDtypeStruct((S, WIDTH), jnp.bfloat16),
        ),
        in_specs=[
            pl.BlockSpec(memory_space=pltpu.HBM),
            pl.BlockSpec(memory_space=pltpu.HBM),
            pl.BlockSpec(memory_space=pltpu.HBM),
        ],
        out_specs=(pl.BlockSpec(memory_space=VMEM), pl.BlockSpec(memory_space=VMEM)),
        scratch_shapes=[
            pltpu.SMEM((ATOMS,), jnp.int32),
            VMEM((ROWS, WIDTH), jnp.bfloat16),
            VMEM((2, ROWS + 16, 128), jnp.float32),
            VMEM((ROWS, WIDTH), jnp.bfloat16),
            VMEM((4, 256, ROWS), jnp.bfloat16),
            VMEM((4, 2, WIDTH + 16, BLOCK), jnp.int16),
            VMEM((7, WIDTH + 16, BLOCK), jnp.int16),
            VMEM((8, BLOCK), jnp.float32),
            VMEM((15, 8, BLOCK), jnp.float32),
            VMEM((16, 8, BLOCK), jnp.float32),
            VMEM((WIDTH + 16, BLOCK), jnp.int16),
            VMEM((WIDTH + 16, BLOCK), jnp.int16),
            VMEM((BLOCK, WIDTH), jnp.bfloat16),
            VMEM((WIDTH, BLOCK), jnp.bfloat16),
            DMA, DMA((CHUNKS,)), DMA((4,)),
            DMA((7,)), DMA((7,)),
            DMA((15,)), DMA((15,)),
            DMA((14,)), DMA((16,)),
            DMA((7,)), DMA((7,)),
            DMA, DMA,
            DMA((7,)), DMA((7,)),
            DMA((8,)), DMA((8,)),
        ],
        compiler_params=pltpu.CompilerParams(
            collective_id=0, has_side_effects=True, vmem_limit_bytes=52 * 2**20
        ),
    )(atom_slot, modes_panel, velocities)


def correlate_kernel(lag_ref, rows_ref, cols_ref, out_hbm, padded, shifted, held, out_sem):
    for h in range(2):
        padded[h, :S, :] = cols_ref[:, h * 128 : (h + 1) * 128].astype(jnp.float32)
        padded[h, S:, :] = jnp.zeros((MAXLAG, 128), jnp.float32)
    copies = []
    for i in range(LAGS):
        lag = lag_ref[i]
        for h in range(2):
            cut = padded[h, pl.ds(lag, S), :].astype(jnp.bfloat16)
            shifted[i % 2, :, h * 128 : (h + 1) * 128] = cut
        factor = lax.rsqrt(jnp.broadcast_to((S - lag).astype(jnp.float32), (1, WIDTH)))
        for p in range(2):
            rows = pl.ds(p * WIDTH, WIDTH)
            product = jnp.dot(
                rows_ref[rows, :], shifted[i % 2], preferred_element_type=jnp.float32
            )
            held[i, rows, :] = product * factor
        copies.append(pltpu.make_async_copy(held.at[i], out_hbm.at[i], out_sem.at[i]))
        copies[-1].start()
    for copy in copies:
        copy.wait()


def correlate(row_modes, column_modes, lag_offsets):
    return pl.pallas_call(
        correlate_kernel,
        out_shape=jax.ShapeDtypeStruct((LAGS, 2 * WIDTH, WIDTH), jnp.float32),
        in_specs=[
            pl.BlockSpec(memory_space=pltpu.SMEM),
            pl.BlockSpec(memory_space=VMEM),
            pl.BlockSpec(memory_space=VMEM),
        ],
        out_specs=pl.BlockSpec(memory_space=pl.ANY),
        scratch_shapes=[
            VMEM((2, S + MAXLAG, 128), jnp.float32),
            VMEM((2, S, WIDTH), jnp.bfloat16),
            VMEM((LAGS, 2 * WIDTH, WIDTH), jnp.float32),
            DMA((LAGS,)),
        ],
        compiler_params=pltpu.CompilerParams(vmem_limit_bytes=24 * 2**20),
    )(lag_offsets, row_modes, column_modes)


def local(velocities, modes_panel, atom_slot, lag_offsets):
    row_modes, column_modes = project(velocities, modes_panel, atom_slot)
    return correlate(row_modes, column_modes, lag_offsets)


def solution(mesh):
    return jax.shard_map(
        local,
        mesh=mesh,
        in_specs=(P(None, "row"), P("row", "col"), P("row"), P()),
        out_specs=P(None, "row", "col"),
        check_vma=False,
    )
```

```python
import jax
import jax.numpy as jnp
from jax import lax
from jax.experimental import pallas as pl
from jax.experimental.pallas import tpu as pltpu
from jax.sharding import PartitionSpec as P

M = 4096
LAGS = 8
MAXLAG = 256
S = 1024
ATOMS = 2560
ROWS = 3 * ATOMS
WIDTH = 256
BLOCK = 128
CHUNKS = 4
UNIT = 16
TINY = 1e-30
FULL = 32760.0
epsilon = 1e-06

MESH = pl.DeviceIdType.MESH
VMEM = pltpu.VMEM
DMA = pltpu.SemaphoreType.DMA


def code(values):
    top = jnp.max(jnp.abs(values), axis=0, keepdims=True)
    power = jnp.ceil(jnp.log2(jnp.maximum(top, TINY)))
    coded = jnp.round(values * (FULL * jnp.exp2(-power)))
    powers = jnp.broadcast_to(power, (16, values.shape[1]))
    return coded.astype(jnp.int32).astype(jnp.int16), powers.astype(jnp.int32).astype(jnp.int16)


def decode(ref):
    power = ref[WIDTH:, :].astype(jnp.int32).astype(jnp.float32)[0:1, :]
    return ref[:WIDTH, :].astype(jnp.int32).astype(jnp.float32) * (jnp.exp2(power) / FULL)


def project_kernel(
    slot_hbm, panel_hbm, v_hbm, row_out, col_out,
    slot_ref, panel, wide, ordered, v_buf, part, sent, landed, energy_send, energy_land, there_land, t_sent, t_land, block_n, moved,
    slot_sem, panel_sem, v_sem, rs_send, rs_recv, e_send, e_recv, there_send, there_recv, c_send, c_recv, t_send, t_recv,
    b_send, b_recv, s_send, s_recv,
):
    r, c = lax.axis_index("row"), lax.axis_index("col")
    y, z = r // 2, r % 2
    chip, core = c // 2, c % 2
    zh, x = chip // 4, chip % 4

    slot_copy = pltpu.make_async_copy(slot_hbm, slot_ref, slot_sem)
    slot_copy.start()
    piece = ROWS // CHUNKS
    panel_copies = []
    for i in range(CHUNKS):
        rows = pl.ds(i * piece, piece)
        panel_copies.append(
            pltpu.make_async_copy(panel_hbm.at[rows, :], panel.at[rows, :], panel_sem.at[i])
        )
        panel_copies[-1].start()
    quads = [lax.rem(y + i + 1, 4) for i in range(4)]
    v_copies = []
    for i, q in enumerate(quads):
        rows = pl.ds(pl.multiple_of(q * 256, 256), 256)
        v_copies.append(pltpu.make_async_copy(v_hbm.at[rows, :], v_buf.at[i], v_sem.at[i]))

    barrier = pltpu.get_barrier_semaphore()
    for d in range(1, 8):
        pl.semaphore_signal(barrier, inc=1, device_id=(lax.rem(r + d, 8), c), device_id_type=MESH)
    for d in range(1, 16):
        pl.semaphore_signal(barrier, inc=1, device_id=(r, lax.rem(c + d, 16)), device_id_type=MESH)
    partner = (chip, 2 * r + core)
    moves = chip != r

    @pl.when(moves)
    def _():
        for k in range(16):
            pl.semaphore_signal(barrier, inc=1, device_id=(chip, k), device_id_type=MESH)

    for i in range(CHUNKS):
        panel_copies[i].wait()
        if i == CHUNKS - 1:
            for copy in v_copies:
                copy.start()

        def widen(n, _, i=i):
            start = pl.multiple_of(i * piece + n * 64, 64)
            v = panel[pl.ds(start, 64), :].astype(jnp.float32)
            wide[0, pl.ds(8 + start, 64), :] = v[:, :128]
            wide[1, pl.ds(8 + start, 64), :] = v[:, 128:]
            return 0

        lax.fori_loop(0, piece // 64, widen, 0)
    slot_copy.wait()
    sub = lax.broadcasted_iota(jnp.int32, (8, 128), 0)

    def take(g, _):
        base = [3 * slot_ref[g * UNIT + u] + 8 for u in range(UNIT)]
        for h in range(2):
            tiles = []
            for t in range(3 * UNIT // 8):
                tile = None
                for u in range(UNIT):
                    low = 3 * u - 8 * t
                    if low <= -3 or low >= 8:
                        continue
                    v = wide[h, pl.ds(base[u] - low, 8), :]
                    tile = v if tile is None else jnp.where(sub >= low, v, tile)
                tiles.append(tile)
            for t in range(0, len(tiles), 2):
                both = jnp.concatenate([tiles[t], tiles[t + 1]], axis=0).astype(jnp.bfloat16)
                at = pl.multiple_of(g * (3 * UNIT) + t * 8, 16)
                ordered[pl.ds(at, 16), h * 128 : (h + 1) * 128] = both
        return 0

    lax.fori_loop(0, ATOMS // UNIT, take, 0)

    pl.semaphore_wait(barrier, 36)

    def rs_copy(i, zz):
        to_z = lax.rem(z + 1 + zz, 2)
        k = 2 * i + zz
        return pltpu.make_async_remote_copy(
            src_ref=sent.at[i, to_z], dst_ref=landed.at[k],
            send_sem=rs_send.at[k], recv_sem=rs_recv.at[k],
            device_id=(2 * lax.rem(y + i + 1, 4) + to_z, c), device_id_type=MESH,
        )

    def step(i, _):
        pltpu.make_async_copy(v_hbm.at[pl.ds(0, 256), :], v_buf.at[i], v_sem.at[i]).wait()
        part[i] = jnp.dot(v_buf[i], ordered[...], preferred_element_type=jnp.float32)
        for zz in range(2):
            coded, powers = code(part[i, zz * BLOCK : (zz + 1) * BLOCK, :].T)
            sent[i, zz, :WIDTH, :] = coded
            sent[i, zz, WIDTH:, :] = powers
        rs_copy(i, 0).start()

        @pl.when(i < 3)
        def _():
            rs_copy(i, 1).start()

        return 0

    lax.fori_loop(0, 4, step, 0)
    rs_copies = [rs_copy(k // 2, k % 2) for k in range(7)]
    turned = part[3, pl.ds(pl.multiple_of(z * BLOCK, BLOCK), BLOCK), :].T
    for k in range(7):
        rs_copies[k].wait_recv()
        turned = turned + decode(landed.at[k])

    t_sent[:WIDTH, :], t_sent[WIDTH:, :] = code(turned)
    t_copy = pltpu.make_async_remote_copy(
        src_ref=t_sent, dst_ref=t_land, send_sem=t_send, recv_sem=t_recv,
        device_id=partner, device_id_type=MESH,
    )

    @pl.when(moves)
    def _():
        t_copy.start()

    own = jnp.sum(turned * turned, axis=0, keepdims=True)
    energy_send[...] = jnp.broadcast_to(own, (8, BLOCK))
    e_copies = []
    for d in range(1, 8):
        for k in range(2):
            n = 2 * (d - 1) + k
            copy = pltpu.make_async_remote_copy(
                src_ref=energy_send, dst_ref=there_land.at[c],
                send_sem=there_send.at[n], recv_sem=there_recv.at[c],
                device_id=(lax.rem(r + d, 8), 2 * r + k), device_id_type=MESH,
            )
            copy.start()
            e_copies.append(copy)
    own_copies = []
    for d in range(1, 16):
        copy = pltpu.make_async_remote_copy(
            src_ref=energy_send, dst_ref=energy_land.at[d - 1],
            send_sem=e_send.at[d - 1], recv_sem=e_recv.at[d - 1],
            device_id=(r, lax.rem(c + d, 16)), device_id_type=MESH,
        )
        copy.start()
        own_copies.append(copy)
    e_copies += own_copies
    total = own
    for d in range(15):
        own_copies[d].wait_recv()
        total = total + energy_land[d, 0:1, :]
    scaled = turned * lax.rsqrt(total / M + epsilon)
    block_n[...] = scaled.T.astype(jnp.bfloat16)

    def rows_of(of_row):
        return pl.ds(pl.multiple_of(of_row * BLOCK, BLOCK), BLOCK)

    def place(of_chip):
        return (
            pl.ds(pl.multiple_of(core * WIDTH, WIDTH), WIDTH),
            pl.ds(pl.multiple_of(of_chip * BLOCK, BLOCK), BLOCK),
        )

    def to_row(k, src, rows, device):
        copy = pltpu.make_async_remote_copy(
            src_ref=src, dst_ref=col_out.at[rows, :],
            send_sem=c_send.at[k], recv_sem=c_recv.at[k],
            device_id=(device, c), device_id_type=MESH,
        )
        copy.start()
        return copy

    def to_col(k, src, spot, chip_to):
        copy = pltpu.make_async_remote_copy(
            src_ref=src, dst_ref=row_out.at[spot],
            send_sem=b_send.at[k], recv_sem=b_recv.at[k],
            device_id=(r, 2 * chip_to + core), device_id_type=MESH,
        )
        copy.start()
        return copy

    def to_sibling(k, src, spot):
        copy = pltpu.make_async_remote_copy(
            src_ref=src, dst_ref=row_out.at[spot],
            send_sem=s_send.at[k], recv_sem=s_recv.at[k],
            device_id=(r, 2 * chip + 1 - core), device_id_type=MESH,
        )
        copy.start()
        return copy

    c_copies = [to_row(0, block_n, rows_of(r), 2 * y + 1 - z)]
    col_out[rows_of(r), :] = block_n[...]

    @pl.when(moves)
    def _():
        energy = jnp.zeros((1, BLOCK), jnp.float32)
        for k in range(16):
            pltpu.make_async_remote_copy(
                src_ref=energy_send, dst_ref=there_land.at[k],
                send_sem=there_send.at[0], recv_sem=there_recv.at[k],
                device_id=partner, device_id_type=MESH,
            ).wait_recv()
            energy = energy + there_land[k, 0:1, :]
        t_copy.wait_recv()
        moved[...] = (decode(t_land) * lax.rsqrt(energy / M + epsilon)).astype(jnp.bfloat16)

    @pl.when(jnp.logical_not(moves))
    def _():
        moved[...] = scaled.astype(jnp.bfloat16)

    far = 4 * (1 - zh)
    near = 4 * zh
    b_copies = [to_col(0, moved, place(chip), far + x)]
    for d in (2, 1, 3):
        b_copies.append(to_col(d, moved, place(chip), near + lax.rem(x + d, 4)))
    for d in (2, 1, 3):
        c_copies.append(to_row(d, block_n, rows_of(r), 2 * lax.rem(y + d, 4) + z))
    s_copies = [to_sibling(0, moved, place(chip))]
    row_out[place(chip)] = moved[...]
    b_copies[0].wait_recv()
    other = place(far + x)
    for d in (2, 1, 3):
        b_copies.append(to_col(3 + d, row_out.at[other], other, near + lax.rem(x + d, 4)))
    c_copies[0].wait_recv()
    beside = rows_of(2 * y + 1 - z)
    for d in (2, 1, 3):
        c_copies.append(to_row(3 + d, col_out.at[beside, :], beside, 2 * lax.rem(y + d, 4) + z))
    s_copies.append(to_sibling(1, row_out.at[other], other))
    for n, side in enumerate((near, far)):
        for m, d in enumerate((2, 1, 3)):
            b_copies[1 + 3 * n + m].wait_recv()
            spot = place(side + lax.rem(x + 4 - d, 4))
            s_copies.append(to_sibling(2 + 3 * n + m, row_out.at[spot], spot))
    for copy in (*s_copies, *c_copies[1:]):
        copy.wait_recv()

    for copy in (*rs_copies, *e_copies, *c_copies, *b_copies, *s_copies):
        copy.wait_send()

    @pl.when(moves)
    def _():
        t_copy.wait_send()


def project(velocities, modes_panel, atom_slot):
    return pl.pallas_call(
        project_kernel,
        out_shape=(
            jax.ShapeDtypeStruct((2 * WIDTH, S), jnp.bfloat16),
            jax.ShapeDtypeStruct((S, WIDTH), jnp.bfloat16),
        ),
        in_specs=[
            pl.BlockSpec(memory_space=pltpu.HBM),
            pl.BlockSpec(memory_space=pltpu.HBM),
            pl.BlockSpec(memory_space=pltpu.HBM),
        ],
        out_specs=(pl.BlockSpec(memory_space=VMEM), pl.BlockSpec(memory_space=VMEM)),
        scratch_shapes=[
            pltpu.SMEM((ATOMS,), jnp.int32),
            VMEM((ROWS, WIDTH), jnp.bfloat16),
            VMEM((2, ROWS + 16, 128), jnp.float32),
            VMEM((ROWS, WIDTH), jnp.bfloat16),
            VMEM((4, 256, ROWS), jnp.bfloat16),
            VMEM((4, 2 * BLOCK, WIDTH), jnp.float32),
            VMEM((4, 2, WIDTH + 16, BLOCK), jnp.int16),
            VMEM((7, WIDTH + 16, BLOCK), jnp.int16),
            VMEM((8, BLOCK), jnp.float32),
            VMEM((15, 8, BLOCK), jnp.float32),
            VMEM((16, 8, BLOCK), jnp.float32),
            VMEM((WIDTH + 16, BLOCK), jnp.int16),
            VMEM((WIDTH + 16, BLOCK), jnp.int16),
            VMEM((BLOCK, WIDTH), jnp.bfloat16),
            VMEM((WIDTH, BLOCK), jnp.bfloat16),
            DMA, DMA((CHUNKS,)), DMA((4,)),
            DMA((7,)), DMA((7,)),
            DMA((15,)), DMA((15,)),
            DMA((14,)), DMA((16,)),
            DMA((7,)), DMA((7,)),
            DMA, DMA,
            DMA((7,)), DMA((7,)),
            DMA((8,)), DMA((8,)),
        ],
        compiler_params=pltpu.CompilerParams(
            collective_id=0, has_side_effects=True, vmem_limit_bytes=52 * 2**20
        ),
    )(atom_slot, modes_panel, velocities)


def correlate_kernel(lag_ref, rows_ref, cols_ref, out_hbm, padded, shifted, held, out_sem):
    for h in range(2):
        padded[h, :S, :] = cols_ref[:, h * 128 : (h + 1) * 128].astype(jnp.float32)
        padded[h, S:, :] = jnp.zeros((MAXLAG, 128), jnp.float32)
    copies = []
    for i in range(LAGS):
        lag = lag_ref[i]
        for h in range(2):
            cut = padded[h, pl.ds(lag, S), :].astype(jnp.bfloat16)
            shifted[i % 2, :, h * 128 : (h + 1) * 128] = cut
        factor = lax.rsqrt(jnp.broadcast_to((S - lag).astype(jnp.float32), (1, WIDTH)))
        for p in range(2):
            rows = pl.ds(p * WIDTH, WIDTH)
            product = jnp.dot(
                rows_ref[rows, :], shifted[i % 2], preferred_element_type=jnp.float32
            )
            held[i, rows, :] = product * factor
        copies.append(pltpu.make_async_copy(held.at[i], out_hbm.at[i], out_sem.at[i]))
        copies[-1].start()
    for copy in copies:
        copy.wait()


def correlate(row_modes, column_modes, lag_offsets):
    return pl.pallas_call(
        correlate_kernel,
        out_shape=jax.ShapeDtypeStruct((LAGS, 2 * WIDTH, WIDTH), jnp.float32),
        in_specs=[
            pl.BlockSpec(memory_space=pltpu.SMEM),
            pl.BlockSpec(memory_space=VMEM),
            pl.BlockSpec(memory_space=VMEM),
        ],
        out_specs=pl.BlockSpec(memory_space=pl.ANY),
        scratch_shapes=[
            VMEM((2, S + MAXLAG, 128), jnp.float32),
            VMEM((2, S, WIDTH), jnp.bfloat16),
            VMEM((LAGS, 2 * WIDTH, WIDTH), jnp.float32),
            DMA((LAGS,)),
        ],
        compiler_params=pltpu.CompilerParams(vmem_limit_bytes=24 * 2**20),
    )(lag_offsets, row_modes, column_modes)


def local(velocities, modes_panel, atom_slot, lag_offsets):
    row_modes, column_modes = project(velocities, modes_panel, atom_slot)
    return correlate(row_modes, column_modes, lag_offsets)


def solution(mesh):
    return jax.shard_map(
        local,
        mesh=mesh,
        in_specs=(P(None, "row"), P("row", "col"), P("row"), P()),
        out_specs=P(None, "row", "col"),
        check_vma=False,
    )
```

```python
import jax
import jax.numpy as jnp
from jax import lax
from jax.experimental import pallas as pl
from jax.experimental.pallas import tpu as pltpu
from jax.sharding import PartitionSpec as P

M = 4096
LAGS = 8
MAXLAG = 256
S = 1024
ATOMS = 2560
ROWS = 3 * ATOMS
WIDTH = 256
BLOCK = 128
CHUNKS = 4
UNIT = 16
TINY = 1e-30
FULL = 32760.0
epsilon = 1e-06

MESH = pl.DeviceIdType.MESH
VMEM = pltpu.VMEM
DMA = pltpu.SemaphoreType.DMA


def code(values):
    top = jnp.max(jnp.abs(values), axis=0, keepdims=True)
    power = jnp.ceil(jnp.log2(jnp.maximum(top, TINY)))
    coded = jnp.round(values * (FULL * jnp.exp2(-power)))
    powers = jnp.broadcast_to(power, (16, values.shape[1]))
    return coded.astype(jnp.int32).astype(jnp.int16), powers.astype(jnp.int32).astype(jnp.int16)


def decode(ref):
    power = ref[WIDTH:, :].astype(jnp.int32).astype(jnp.float32)[0:1, :]
    return ref[:WIDTH, :].astype(jnp.int32).astype(jnp.float32) * (jnp.exp2(power) / FULL)


def project_kernel(
    slot_hbm, panel_hbm, v_hbm, row_out, col_out,
    slot_ref, panel, wide, ordered, v_buf, part, sent, landed, energy_send, energy_land, there_land, there_sum, t_sent, t_land, block_n, moved,
    slot_sem, panel_sem, v_sem, rs_send, rs_recv, e_send, e_recv, there_send, there_recv, c_send, c_recv, t_send, t_recv,
    b_send, b_recv, s_send, s_recv,
):
    r, c = lax.axis_index("row"), lax.axis_index("col")
    y, z = r // 2, r % 2
    chip, core = c // 2, c % 2
    zh, x = chip // 4, chip % 4

    slot_copy = pltpu.make_async_copy(slot_hbm, slot_ref, slot_sem)
    slot_copy.start()
    piece = ROWS // CHUNKS
    panel_copies = []
    for i in range(CHUNKS):
        rows = pl.ds(i * piece, piece)
        panel_copies.append(
            pltpu.make_async_copy(panel_hbm.at[rows, :], panel.at[rows, :], panel_sem.at[i])
        )
        panel_copies[-1].start()
    quads = [lax.rem(y + i + 1, 4) for i in range(4)]
    v_copies = []
    for i, q in enumerate(quads):
        rows = pl.ds(pl.multiple_of(q * 256, 256), 256)
        v_copies.append(pltpu.make_async_copy(v_hbm.at[rows, :], v_buf.at[i], v_sem.at[i]))

    barrier = pltpu.get_barrier_semaphore()
    for d in range(1, 8):
        pl.semaphore_signal(barrier, inc=1, device_id=(lax.rem(r + d, 8), c), device_id_type=MESH)
    for d in range(1, 16):
        pl.semaphore_signal(barrier, inc=1, device_id=(r, lax.rem(c + d, 16)), device_id_type=MESH)
    target = (chip, 2 * lax.rem(r + chip, 8) + core)
    origin = lax.rem(chip + 8 - r, 8)
    moves = (r != 0) | (chip != 0)
    elsewhere = origin != r

    @pl.when(elsewhere)
    def _():
        for k in range(16):
            pl.semaphore_signal(barrier, inc=1, device_id=(origin, k), device_id_type=MESH)

    for i in range(CHUNKS):
        panel_copies[i].wait()
        if i == CHUNKS - 1:
            for copy in v_copies:
                copy.start()

        def widen(n, _, i=i):
            start = pl.multiple_of(i * piece + n * 64, 64)
            v = panel[pl.ds(start, 64), :].astype(jnp.float32)
            wide[0, pl.ds(8 + start, 64), :] = v[:, :128]
            wide[1, pl.ds(8 + start, 64), :] = v[:, 128:]
            return 0

        lax.fori_loop(0, piece // 64, widen, 0)
    slot_copy.wait()
    sub = lax.broadcasted_iota(jnp.int32, (8, 128), 0)

    def take(g, _):
        base = [3 * slot_ref[g * UNIT + u] + 8 for u in range(UNIT)]
        for h in range(2):
            tiles = []
            for t in range(3 * UNIT // 8):
                tile = None
                for u in range(UNIT):
                    low = 3 * u - 8 * t
                    if low <= -3 or low >= 8:
                        continue
                    v = wide[h, pl.ds(base[u] - low, 8), :]
                    tile = v if tile is None else jnp.where(sub >= low, v, tile)
                tiles.append(tile)
            for t in range(0, len(tiles), 2):
                both = jnp.concatenate([tiles[t], tiles[t + 1]], axis=0).astype(jnp.bfloat16)
                at = pl.multiple_of(g * (3 * UNIT) + t * 8, 16)
                ordered[pl.ds(at, 16), h * 128 : (h + 1) * 128] = both
        return 0

    lax.fori_loop(0, ATOMS // UNIT, take, 0)

    pl.semaphore_wait(barrier, 36)

    def rs_copy(i, zz):
        to_z = lax.rem(z + 1 + zz, 2)
        k = 2 * i + zz
        return pltpu.make_async_remote_copy(
            src_ref=sent.at[i, to_z], dst_ref=landed.at[k],
            send_sem=rs_send.at[k], recv_sem=rs_recv.at[k],
            device_id=(2 * lax.rem(y + i + 1, 4) + to_z, c), device_id_type=MESH,
        )

    def step(i, _):
        pltpu.make_async_copy(v_hbm.at[pl.ds(0, 256), :], v_buf.at[i], v_sem.at[i]).wait()
        part[i] = jnp.dot(v_buf[i], ordered[...], preferred_element_type=jnp.float32)
        for zz in range(2):
            coded, powers = code(part[i, zz * BLOCK : (zz + 1) * BLOCK, :].T)
            sent[i, zz, :WIDTH, :] = coded
            sent[i, zz, WIDTH:, :] = powers
        rs_copy(i, 0).start()

        @pl.when(i < 3)
        def _():
            rs_copy(i, 1).start()

        return 0

    lax.fori_loop(0, 4, step, 0)
    rs_copies = [rs_copy(k // 2, k % 2) for k in range(7)]
    turned = part[3, pl.ds(pl.multiple_of(z * BLOCK, BLOCK), BLOCK), :].T
    for k in range(7):
        rs_copies[k].wait_recv()
        turned = turned + decode(landed.at[k])

    t_sent[:WIDTH, :], t_sent[WIDTH:, :] = code(turned)
    t_copy = pltpu.make_async_remote_copy(
        src_ref=t_sent, dst_ref=t_land, send_sem=t_send, recv_sem=t_recv,
        device_id=target, device_id_type=MESH,
    )

    @pl.when(moves)
    def _():
        t_copy.start()

    own = jnp.sum(turned * turned, axis=0, keepdims=True)
    energy_send[...] = jnp.broadcast_to(own, (8, BLOCK))
    e_copies = []
    for d in range(1, 8):
        to_row_of = lax.rem(r + d, 8)
        for k in range(2):
            n = 2 * (d - 1) + k
            copy = pltpu.make_async_remote_copy(
                src_ref=energy_send, dst_ref=there_land.at[c],
                send_sem=there_send.at[n], recv_sem=there_recv.at[c],
                device_id=(to_row_of, 2 * lax.rem(to_row_of + r, 8) + k), device_id_type=MESH,
            )
            copy.start()
            e_copies.append(copy)
    own_copies = []
    for d in range(1, 16):
        copy = pltpu.make_async_remote_copy(
            src_ref=energy_send, dst_ref=energy_land.at[d - 1],
            send_sem=e_send.at[d - 1], recv_sem=e_recv.at[d - 1],
            device_id=(r, lax.rem(c + d, 16)), device_id_type=MESH,
        )
        copy.start()
        own_copies.append(copy)
    e_copies += own_copies
    total = own
    for d in range(15):
        own_copies[d].wait_recv()
        total = total + energy_land[d, 0:1, :]
    scaled = turned * lax.rsqrt(total / M + epsilon)
    block_n[...] = scaled.T.astype(jnp.bfloat16)

    def rows_of(of_row):
        return pl.ds(pl.multiple_of(of_row * BLOCK, BLOCK), BLOCK)

    def place(of_chip):
        of_row = lax.rem(of_chip + 8 - r, 8)
        return (
            pl.ds(pl.multiple_of(core * WIDTH, WIDTH), WIDTH),
            pl.ds(pl.multiple_of(of_row * BLOCK, BLOCK), BLOCK),
        )

    def to_row(k, src, rows, device):
        copy = pltpu.make_async_remote_copy(
            src_ref=src, dst_ref=col_out.at[rows, :],
            send_sem=c_send.at[k], recv_sem=c_recv.at[k],
            device_id=(device, c), device_id_type=MESH,
        )
        copy.start()
        return copy

    def to_col(k, src, spot, chip_to):
        copy = pltpu.make_async_remote_copy(
            src_ref=src, dst_ref=row_out.at[spot],
            send_sem=b_send.at[k], recv_sem=b_recv.at[k],
            device_id=(r, 2 * chip_to + core), device_id_type=MESH,
        )
        copy.start()
        return copy

    def to_sibling(k, src, spot):
        copy = pltpu.make_async_remote_copy(
            src_ref=src, dst_ref=row_out.at[spot],
            send_sem=s_send.at[k], recv_sem=s_recv.at[k],
            device_id=(r, 2 * chip + 1 - core), device_id_type=MESH,
        )
        copy.start()
        return copy

    c_copies = [to_row(0, block_n, rows_of(r), 2 * y + 1 - z)]
    col_out[rows_of(r), :] = block_n[...]

    there_sum[...] = total

    @pl.when(elsewhere)
    def _():
        energy = jnp.zeros((1, BLOCK), jnp.float32)
        for k in range(16):
            pltpu.make_async_remote_copy(
                src_ref=energy_send, dst_ref=there_land.at[k],
                send_sem=there_send.at[0], recv_sem=there_recv.at[k],
                device_id=target, device_id_type=MESH,
            ).wait_recv()
            energy = energy + there_land[k, 0:1, :]
        there_sum[...] = energy

    @pl.when(moves)
    def _():
        t_copy.wait_recv()
        factor = lax.rsqrt(there_sum[...] / M + epsilon)
        moved[...] = (decode(t_land) * factor).astype(jnp.bfloat16)

    @pl.when(jnp.logical_not(moves))
    def _():
        moved[...] = scaled.astype(jnp.bfloat16)

    far = 4 * (1 - zh)
    near = 4 * zh
    b_copies = [to_col(0, moved, place(chip), far + x)]
    for d in (2, 1, 3):
        b_copies.append(to_col(d, moved, place(chip), near + lax.rem(x + d, 4)))
    for d in (2, 1, 3):
        c_copies.append(to_row(d, block_n, rows_of(r), 2 * lax.rem(y + d, 4) + z))
    s_copies = [to_sibling(0, moved, place(chip))]
    row_out[place(chip)] = moved[...]
    b_copies[0].wait_recv()
    other = place(far + x)
    for d in (2, 1, 3):
        b_copies.append(to_col(3 + d, row_out.at[other], other, near + lax.rem(x + d, 4)))
    c_copies[0].wait_recv()
    beside = rows_of(2 * y + 1 - z)
    for d in (2, 1, 3):
        c_copies.append(to_row(3 + d, col_out.at[beside, :], beside, 2 * lax.rem(y + d, 4) + z))
    s_copies.append(to_sibling(1, row_out.at[other], other))
    for n, side in enumerate((near, far)):
        for m, d in ((1, 1), (2, 3), (0, 2)):
            b_copies[1 + 3 * n + m].wait_recv()
            spot = place(side + lax.rem(x + 4 - d, 4))
            s_copies.append(to_sibling(2 + 3 * n + m, row_out.at[spot], spot))
    for copy in (*s_copies, *c_copies[1:]):
        copy.wait_recv()

    for copy in (*rs_copies, *e_copies, *c_copies, *b_copies, *s_copies):
        copy.wait_send()

    @pl.when(moves)
    def _():
        t_copy.wait_send()


def project(velocities, modes_panel, atom_slot):
    return pl.pallas_call(
        project_kernel,
        out_shape=(
            jax.ShapeDtypeStruct((2 * WIDTH, S), jnp.bfloat16),
            jax.ShapeDtypeStruct((S, WIDTH), jnp.bfloat16),
        ),
        in_specs=[
            pl.BlockSpec(memory_space=pltpu.HBM),
            pl.BlockSpec(memory_space=pltpu.HBM),
            pl.BlockSpec(memory_space=pltpu.HBM),
        ],
        out_specs=(pl.BlockSpec(memory_space=VMEM), pl.BlockSpec(memory_space=VMEM)),
        scratch_shapes=[
            pltpu.SMEM((ATOMS,), jnp.int32),
            VMEM((ROWS, WIDTH), jnp.bfloat16),
            VMEM((2, ROWS + 16, 128), jnp.float32),
            VMEM((ROWS, WIDTH), jnp.bfloat16),
            VMEM((4, 256, ROWS), jnp.bfloat16),
            VMEM((4, 2 * BLOCK, WIDTH), jnp.float32),
            VMEM((4, 2, WIDTH + 16, BLOCK), jnp.int16),
            VMEM((7, WIDTH + 16, BLOCK), jnp.int16),
            VMEM((8, BLOCK), jnp.float32),
            VMEM((15, 8, BLOCK), jnp.float32),
            VMEM((16, 8, BLOCK), jnp.float32),
            VMEM((1, BLOCK), jnp.float32),
            VMEM((WIDTH + 16, BLOCK), jnp.int16),
            VMEM((WIDTH + 16, BLOCK), jnp.int16),
            VMEM((BLOCK, WIDTH), jnp.bfloat16),
            VMEM((WIDTH, BLOCK), jnp.bfloat16),
            DMA, DMA((CHUNKS,)), DMA((4,)),
            DMA((7,)), DMA((7,)),
            DMA((15,)), DMA((15,)),
            DMA((14,)), DMA((16,)),
            DMA((7,)), DMA((7,)),
            DMA, DMA,
            DMA((7,)), DMA((7,)),
            DMA((8,)), DMA((8,)),
        ],
        compiler_params=pltpu.CompilerParams(
            collective_id=0, has_side_effects=True, vmem_limit_bytes=52 * 2**20
        ),
    )(atom_slot, modes_panel, velocities)


def correlate_kernel(lag_ref, rows_ref, cols_ref, out_hbm, padded, shifted, held, out_sem):
    for h in range(2):
        padded[h, :S, :] = cols_ref[:, h * 128 : (h + 1) * 128].astype(jnp.float32)
        padded[h, S:, :] = jnp.zeros((MAXLAG, 128), jnp.float32)
    copies = []
    for i in range(LAGS):
        lag = lag_ref[i]
        for h in range(2):
            cut = padded[h, pl.ds(lag, S), :].astype(jnp.bfloat16)
            shifted[i % 2, :, h * 128 : (h + 1) * 128] = cut
        factor = lax.rsqrt(jnp.broadcast_to((S - lag).astype(jnp.float32), (1, WIDTH)))
        for p in range(2):
            rows = pl.ds(p * WIDTH, WIDTH)
            product = jnp.dot(
                rows_ref[rows, :], shifted[i % 2], preferred_element_type=jnp.float32
            )
            held[i, rows, :] = product * factor
        copies.append(pltpu.make_async_copy(held.at[i], out_hbm.at[i], out_sem.at[i]))
        copies[-1].start()
    for copy in copies:
        copy.wait()


def correlate(row_modes, column_modes, lag_offsets):
    return pl.pallas_call(
        correlate_kernel,
        out_shape=jax.ShapeDtypeStruct((LAGS, 2 * WIDTH, WIDTH), jnp.float32),
        in_specs=[
            pl.BlockSpec(memory_space=pltpu.SMEM),
            pl.BlockSpec(memory_space=VMEM),
            pl.BlockSpec(memory_space=VMEM),
        ],
        out_specs=pl.BlockSpec(memory_space=pl.ANY),
        scratch_shapes=[
            VMEM((2, S + MAXLAG, 128), jnp.float32),
            VMEM((2, S, WIDTH), jnp.bfloat16),
            VMEM((LAGS, 2 * WIDTH, WIDTH), jnp.float32),
            DMA((LAGS,)),
        ],
        compiler_params=pltpu.CompilerParams(vmem_limit_bytes=24 * 2**20),
    )(lag_offsets, row_modes, column_modes)


def local(velocities, modes_panel, atom_slot, lag_offsets):
    row_modes, column_modes = project(velocities, modes_panel, atom_slot)
    return correlate(row_modes, column_modes, lag_offsets)


def solution(mesh):
    return jax.shard_map(
        local,
        mesh=mesh,
        in_specs=(P(None, "row"), P("row", "col"), P("row"), P()),
        out_specs=P(None, "row", "col"),
        check_vma=False,
    )
```

```python
import jax
import jax.numpy as jnp
from jax import lax
from jax.experimental import pallas as pl
from jax.experimental.pallas import tpu as pltpu
from jax.sharding import PartitionSpec as P

M = 4096
LAGS = 8
MAXLAG = 256
S = 1024
ATOMS = 2560
ROWS = 3 * ATOMS
WIDTH = 256
BLOCK = 128
CHUNKS = 4
UNIT = 16
TINY = 1e-30
FULL = 32760.0
epsilon = 1e-06

MESH = pl.DeviceIdType.MESH
VMEM = pltpu.VMEM
DMA = pltpu.SemaphoreType.DMA


def code(values):
    top = jnp.max(jnp.abs(values), axis=0, keepdims=True)
    power = jnp.ceil(jnp.log2(jnp.maximum(top, TINY)))
    coded = jnp.round(values * (FULL * jnp.exp2(-power)))
    powers = jnp.broadcast_to(power, (16, values.shape[1]))
    return coded.astype(jnp.int32).astype(jnp.int16), powers.astype(jnp.int32).astype(jnp.int16)


def decode(ref):
    power = ref[WIDTH:, :].astype(jnp.int32).astype(jnp.float32)[0:1, :]
    return ref[:WIDTH, :].astype(jnp.int32).astype(jnp.float32) * (jnp.exp2(power) / FULL)


def turn(i):
    return jnp.where(i == 3, 0, jnp.where(i == 2, 1, i + 2))


def project_kernel(
    slot_hbm, panel_hbm, v_hbm, row_out, col_out,
    slot_ref, panel, wide, ordered, v_buf, part, sent, landed, own_send, own_land, energy_send, energy_land, there_land, there_sum, t_sent, t_land, block_n, moved,
    slot_sem, panel_sem, v_sem, rs_send, rs_recv, pair_send, pair_recv, e_send, e_recv, there_send, there_recv, c_send, c_recv, t_send, t_recv,
    b_send, b_recv, s_send, s_recv,
):
    r, c = lax.axis_index("row"), lax.axis_index("col")
    y, z = r // 2, r % 2
    chip, core = c // 2, c % 2
    zh, x = chip // 4, chip % 4

    slot_copy = pltpu.make_async_copy(slot_hbm, slot_ref, slot_sem)
    slot_copy.start()
    piece = ROWS // CHUNKS
    panel_copies = []
    for i in range(CHUNKS):
        rows = pl.ds(i * piece, piece)
        panel_copies.append(
            pltpu.make_async_copy(panel_hbm.at[rows, :], panel.at[rows, :], panel_sem.at[i])
        )
        panel_copies[-1].start()
    quads = [lax.rem(y + turn(i), 4) for i in range(4)]
    v_copies = []
    for i, q in enumerate(quads):
        rows = pl.ds(pl.multiple_of(q * 256, 256), 256)
        v_copies.append(pltpu.make_async_copy(v_hbm.at[rows, :], v_buf.at[i], v_sem.at[i]))

    barrier = pltpu.get_barrier_semaphore()
    for d in range(1, 8):
        pl.semaphore_signal(barrier, inc=1, device_id=(lax.rem(r + d, 8), c), device_id_type=MESH)
    for d in range(1, 8):
        peer = 2 * lax.rem(chip + d, 8) + core
        pl.semaphore_signal(barrier, inc=1, device_id=(r, peer), device_id_type=MESH)
    sibling = (r, 2 * chip + 1 - core)
    pl.semaphore_signal(barrier, inc=1, device_id=sibling, device_id_type=MESH)
    target = (chip, 2 * lax.rem(r + chip, 8) + core)
    origin = lax.rem(chip + 8 - r, 8)
    moves = (r != 0) | (chip != 0)
    elsewhere = origin != r

    @pl.when(elsewhere)
    def _():
        for k in range(8):
            peer = 2 * k + core
            pl.semaphore_signal(barrier, inc=1, device_id=(origin, peer), device_id_type=MESH)

    for i in range(CHUNKS):
        panel_copies[i].wait()
        if i == CHUNKS - 1:
            for copy in v_copies:
                copy.start()

        def widen(n, _, i=i):
            start = pl.multiple_of(i * piece + n * 64, 64)
            v = panel[pl.ds(start, 64), :].astype(jnp.float32)
            wide[0, pl.ds(8 + start, 64), :] = v[:, :128]
            wide[1, pl.ds(8 + start, 64), :] = v[:, 128:]
            return 0

        lax.fori_loop(0, piece // 64, widen, 0)
    slot_copy.wait()
    sub = lax.broadcasted_iota(jnp.int32, (8, 128), 0)

    def take(g, _):
        base = [3 * slot_ref[g * UNIT + u] + 8 for u in range(UNIT)]
        for h in range(2):
            tiles = []
            for t in range(3 * UNIT // 8):
                tile = None
                for u in range(UNIT):
                    low = 3 * u - 8 * t
                    if low <= -3 or low >= 8:
                        continue
                    v = wide[h, pl.ds(base[u] - low, 8), :]
                    tile = v if tile is None else jnp.where(sub >= low, v, tile)
                tiles.append(tile)
            for t in range(0, len(tiles), 2):
                both = jnp.concatenate([tiles[t], tiles[t + 1]], axis=0).astype(jnp.bfloat16)
                at = pl.multiple_of(g * (3 * UNIT) + t * 8, 16)
                ordered[pl.ds(at, 16), h * 128 : (h + 1) * 128] = both
        return 0

    lax.fori_loop(0, ATOMS // UNIT, take, 0)

    pl.semaphore_wait(barrier, 22)

    def rs_copy(i, zz):
        to_z = lax.rem(z + 1 + zz, 2)
        k = 2 * i + zz
        return pltpu.make_async_remote_copy(
            src_ref=sent.at[i, to_z], dst_ref=landed.at[k],
            send_sem=rs_send.at[k], recv_sem=rs_recv.at[k],
            device_id=(2 * lax.rem(y + turn(i), 4) + to_z, c), device_id_type=MESH,
        )

    def step(i, _):
        pltpu.make_async_copy(v_hbm.at[pl.ds(0, 256), :], v_buf.at[i], v_sem.at[i]).wait()
        part[i] = jnp.dot(v_buf[i], ordered[...], preferred_element_type=jnp.float32)
        for zz in range(2):
            coded, powers = code(part[i, zz * BLOCK : (zz + 1) * BLOCK, :].T)
            sent[i, zz, :WIDTH, :] = coded
            sent[i, zz, WIDTH:, :] = powers
        rs_copy(i, 0).start()

        @pl.when(i < 3)
        def _():
            rs_copy(i, 1).start()

        return 0

    lax.fori_loop(0, 4, step, 0)
    rs_copies = [rs_copy(k // 2, k % 2) for k in range(7)]
    turned = part[3, pl.ds(pl.multiple_of(z * BLOCK, BLOCK), BLOCK), :].T
    for k in range(7):
        rs_copies[k].wait_recv()
        turned = turned + decode(landed.at[k])

    t_sent[:WIDTH, :], t_sent[WIDTH:, :] = code(turned)
    t_copy = pltpu.make_async_remote_copy(
        src_ref=t_sent, dst_ref=t_land, send_sem=t_send, recv_sem=t_recv,
        device_id=target, device_id_type=MESH,
    )

    @pl.when(moves)
    def _():
        t_copy.start()

    own = jnp.sum(turned * turned, axis=0, keepdims=True)
    own_send[...] = jnp.broadcast_to(own, (8, BLOCK))
    pair_copy = pltpu.make_async_remote_copy(
        src_ref=own_send, dst_ref=own_land, send_sem=pair_send, recv_sem=pair_recv,
        device_id=sibling, device_id_type=MESH,
    )
    pair_copy.start()
    pair_copy.wait_recv()
    total = own + own_land[0:1, :]
    energy_send[...] = jnp.broadcast_to(total, (8, BLOCK))
    e_copies = [pair_copy]
    own_copies = []
    for d in range(1, 8):
        copy = pltpu.make_async_remote_copy(
            src_ref=energy_send, dst_ref=energy_land.at[d - 1],
            send_sem=e_send.at[d - 1], recv_sem=e_recv.at[d - 1],
            device_id=(r, 2 * lax.rem(chip + d, 8) + core), device_id_type=MESH,
        )
        copy.start()
        own_copies.append(copy)
        to_row_of = lax.rem(r + d, 8)
        copy = pltpu.make_async_remote_copy(
            src_ref=energy_send, dst_ref=there_land.at[chip],
            send_sem=there_send.at[d - 1], recv_sem=there_recv.at[chip],
            device_id=(to_row_of, 2 * lax.rem(to_row_of + r, 8) + core), device_id_type=MESH,
        )
        copy.start()
        e_copies.append(copy)
    e_copies += own_copies
    for d in range(7):
        own_copies[d].wait_recv()
        total = total + energy_land[d, 0:1, :]
    scaled = turned * lax.rsqrt(total / M + epsilon)
    block_n[...] = scaled.T.astype(jnp.bfloat16)

    def rows_of(of_row):
        return pl.ds(pl.multiple_of(of_row * BLOCK, BLOCK), BLOCK)

    def place(of_chip):
        of_row = lax.rem(of_chip + 8 - r, 8)
        return (
            pl.ds(pl.multiple_of(core * WIDTH, WIDTH), WIDTH),
            pl.ds(pl.multiple_of(of_row * BLOCK, BLOCK), BLOCK),
        )

    def to_row(k, src, rows, device):
        copy = pltpu.make_async_remote_copy(
            src_ref=src, dst_ref=col_out.at[rows, :],
            send_sem=c_send.at[k], recv_sem=c_recv.at[k],
            device_id=(device, c), device_id_type=MESH,
        )
        copy.start()
        return copy

    def to_col(k, src, spot, chip_to):
        copy = pltpu.make_async_remote_copy(
            src_ref=src, dst_ref=row_out.at[spot],
            send_sem=b_send.at[k], recv_sem=b_recv.at[k],
            device_id=(r, 2 * chip_to + core), device_id_type=MESH,
        )
        copy.start()
        return copy

    def to_sibling(k, src, spot):
        copy = pltpu.make_async_remote_copy(
            src_ref=src, dst_ref=row_out.at[spot],
            send_sem=s_send.at[k], recv_sem=s_recv.at[k],
            device_id=sibling, device_id_type=MESH,
        )
        copy.start()
        return copy

    c_copies = [to_row(0, block_n, rows_of(r), 2 * y + 1 - z)]
    col_out[rows_of(r), :] = block_n[...]

    there_sum[...] = total

    @pl.when(elsewhere)
    def _():
        energy = jnp.zeros((1, BLOCK), jnp.float32)
        for k in range(8):
            pltpu.make_async_remote_copy(
                src_ref=energy_send, dst_ref=there_land.at[k],
                send_sem=there_send.at[0], recv_sem=there_recv.at[k],
                device_id=target, device_id_type=MESH,
            ).wait_recv()
            energy = energy + there_land[k, 0:1, :]
        there_sum[...] = energy

    @pl.when(moves)
    def _():
        t_copy.wait_recv()
        factor = lax.rsqrt(there_sum[...] / M + epsilon)
        moved[...] = (decode(t_land) * factor).astype(jnp.bfloat16)

    @pl.when(jnp.logical_not(moves))
    def _():
        moved[...] = scaled.astype(jnp.bfloat16)

    far = 4 * (1 - zh)
    near = 4 * zh
    b_copies = [to_col(0, moved, place(chip), far + x)]
    for d in (2, 1, 3):
        b_copies.append(to_col(d, moved, place(chip), near + lax.rem(x + d, 4)))
    for d in (2, 1, 3):
        c_copies.append(to_row(d, block_n, rows_of(r), 2 * lax.rem(y + d, 4) + z))
    s_copies = [to_sibling(0, moved, place(chip))]
    row_out[place(chip)] = moved[...]
    b_copies[0].wait_recv()
    other = place(far + x)
    for d in (2, 1, 3):
        b_copies.append(to_col(3 + d, row_out.at[other], other, near + lax.rem(x + d, 4)))
    c_copies[0].wait_recv()
    beside = rows_of(2 * y + 1 - z)
    for d in (2, 1, 3):
        c_copies.append(to_row(3 + d, col_out.at[beside, :], beside, 2 * lax.rem(y + d, 4) + z))
    s_copies.append(to_sibling(1, row_out.at[other], other))
    for n, side in enumerate((near, far)):
        for m, d in ((1, 1), (2, 3), (0, 2)):
            b_copies[1 + 3 * n + m].wait_recv()
            spot = place(side + lax.rem(x + 4 - d, 4))
            s_copies.append(to_sibling(2 + 3 * n + m, row_out.at[spot], spot))
    for copy in (*s_copies, *c_copies[1:]):
        copy.wait_recv()

    for copy in (*rs_copies, *e_copies, *c_copies, *b_copies, *s_copies):
        copy.wait_send()

    @pl.when(moves)
    def _():
        t_copy.wait_send()


def project(velocities, modes_panel, atom_slot):
    return pl.pallas_call(
        project_kernel,
        out_shape=(
            jax.ShapeDtypeStruct((2 * WIDTH, S), jnp.bfloat16),
            jax.ShapeDtypeStruct((S, WIDTH), jnp.bfloat16),
        ),
        in_specs=[
            pl.BlockSpec(memory_space=pltpu.HBM),
            pl.BlockSpec(memory_space=pltpu.HBM),
            pl.BlockSpec(memory_space=pltpu.HBM),
        ],
        out_specs=(pl.BlockSpec(memory_space=VMEM), pl.BlockSpec(memory_space=VMEM)),
        scratch_shapes=[
            pltpu.SMEM((ATOMS,), jnp.int32),
            VMEM((ROWS, WIDTH), jnp.bfloat16),
            VMEM((2, ROWS + 16, 128), jnp.float32),
            VMEM((ROWS, WIDTH), jnp.bfloat16),
            VMEM((4, 256, ROWS), jnp.bfloat16),
            VMEM((4, 2 * BLOCK, WIDTH), jnp.float32),
            VMEM((4, 2, WIDTH + 16, BLOCK), jnp.int16),
            VMEM((7, WIDTH + 16, BLOCK), jnp.int16),
            VMEM((8, BLOCK), jnp.float32),
            VMEM((8, BLOCK), jnp.float32),
            VMEM((8, BLOCK), jnp.float32),
            VMEM((7, 8, BLOCK), jnp.float32),
            VMEM((8, 8, BLOCK), jnp.float32),
            VMEM((1, BLOCK), jnp.float32),
            VMEM((WIDTH + 16, BLOCK), jnp.int16),
            VMEM((WIDTH + 16, BLOCK), jnp.int16),
            VMEM((BLOCK, WIDTH), jnp.bfloat16),
            VMEM((WIDTH, BLOCK), jnp.bfloat16),
            DMA, DMA((CHUNKS,)), DMA((4,)),
            DMA((7,)), DMA((7,)),
            DMA, DMA,
            DMA((7,)), DMA((7,)),
            DMA((7,)), DMA((8,)),
            DMA((7,)), DMA((7,)),
            DMA, DMA,
            DMA((7,)), DMA((7,)),
            DMA((8,)), DMA((8,)),
        ],
        compiler_params=pltpu.CompilerParams(
            collective_id=0, has_side_effects=True, vmem_limit_bytes=52 * 2**20
        ),
    )(atom_slot, modes_panel, velocities)


def correlate_kernel(lag_ref, rows_ref, cols_ref, out_hbm, padded, shifted, held, out_sem):
    for h in range(2):
        padded[h, :S, :] = cols_ref[:, h * 128 : (h + 1) * 128].astype(jnp.float32)
        padded[h, S:, :] = jnp.zeros((MAXLAG, 128), jnp.float32)
    copies = []
    for i in range(LAGS):
        lag = lag_ref[i]
        for h in range(2):
            cut = padded[h, pl.ds(lag, S), :].astype(jnp.bfloat16)
            shifted[i % 2, :, h * 128 : (h + 1) * 128] = cut
        factor = lax.rsqrt(jnp.broadcast_to((S - lag).astype(jnp.float32), (1, WIDTH)))
        for p in range(2):
            rows = pl.ds(p * WIDTH, WIDTH)
            product = jnp.dot(
                rows_ref[rows, :], shifted[i % 2], preferred_element_type=jnp.float32
            )
            held[i, rows, :] = product * factor
        copies.append(pltpu.make_async_copy(held.at[i], out_hbm.at[i], out_sem.at[i]))
        copies[-1].start()
    for copy in copies:
        copy.wait()


def correlate(row_modes, column_modes, lag_offsets):
    return pl.pallas_call(
        correlate_kernel,
        out_shape=jax.ShapeDtypeStruct((LAGS, 2 * WIDTH, WIDTH), jnp.float32),
        in_specs=[
            pl.BlockSpec(memory_space=pltpu.SMEM),
            pl.BlockSpec(memory_space=VMEM),
            pl.BlockSpec(memory_space=VMEM),
        ],
        out_specs=pl.BlockSpec(memory_space=pl.ANY),
        scratch_shapes=[
            VMEM((2, S + MAXLAG, 128), jnp.float32),
            VMEM((2, S, WIDTH), jnp.bfloat16),
            VMEM((LAGS, 2 * WIDTH, WIDTH), jnp.float32),
            DMA((LAGS,)),
        ],
        compiler_params=pltpu.CompilerParams(vmem_limit_bytes=24 * 2**20),
    )(lag_offsets, row_modes, column_modes)


def local(velocities, modes_panel, atom_slot, lag_offsets):
    row_modes, column_modes = project(velocities, modes_panel, atom_slot)
    return correlate(row_modes, column_modes, lag_offsets)


def solution(mesh):
    return jax.shard_map(
        local,
        mesh=mesh,
        in_specs=(P(None, "row"), P("row", "col"), P("row"), P()),
        out_specs=P(None, "row", "col"),
        check_vma=False,
    )
```

```python
import jax
import jax.numpy as jnp
from jax import lax
from jax.experimental import pallas as pl
from jax.experimental.pallas import tpu as pltpu
from jax.sharding import PartitionSpec as P

M = 4096
LAGS = 8
MAXLAG = 256
S = 1024
ATOMS = 2560
ROWS = 3 * ATOMS
WIDTH = 256
BLOCK = 128
CHUNKS = 8
UNIT = 16
TINY = 1e-30
FULL = 32760.0
epsilon = 1e-06

MESH = pl.DeviceIdType.MESH
VMEM = pltpu.VMEM
DMA = pltpu.SemaphoreType.DMA


def code(values):
    top = jnp.max(jnp.abs(values), axis=0, keepdims=True)
    power = jnp.ceil(jnp.log2(jnp.maximum(top, TINY)))
    coded = jnp.round(values * (FULL * jnp.exp2(-power)))
    powers = jnp.broadcast_to(power, (16, values.shape[1]))
    return coded.astype(jnp.int32).astype(jnp.int16), powers.astype(jnp.int32).astype(jnp.int16)


def decode(ref):
    power = ref[WIDTH:, :].astype(jnp.int32).astype(jnp.float32)[0:1, :]
    return ref[:WIDTH, :].astype(jnp.int32).astype(jnp.float32) * (jnp.exp2(power) / FULL)


def turn(i):
    return jnp.where(i == 3, 0, jnp.where(i == 2, 1, i + 2))


def project_kernel(
    slot_hbm, panel_hbm, v_hbm, row_out, col_out,
    slot_ref, panel, wide, ordered, v_buf, part, sent, landed, own_send, own_land, energy_send, energy_land, there_land, there_sum, t_sent, t_land, block_n, moved,
    slot_sem, panel_sem, v_sem, rs_send, rs_recv, pair_send, pair_recv, e_send, e_recv, there_send, there_recv, c_send, c_recv, t_send, t_recv,
    b_send, b_recv, s_send, s_recv,
):
    r, c = lax.axis_index("row"), lax.axis_index("col")
    y, z = r // 2, r % 2
    chip, core = c // 2, c % 2
    zh, x = chip // 4, chip % 4

    slot_copy = pltpu.make_async_copy(slot_hbm, slot_ref, slot_sem)
    slot_copy.start()
    piece = ROWS // CHUNKS
    panel_copies = []
    for i in range(CHUNKS):
        rows = pl.ds(i * piece, piece)
        panel_copies.append(
            pltpu.make_async_copy(panel_hbm.at[rows, :], panel.at[rows, :], panel_sem.at[i])
        )
        panel_copies[-1].start()
    quads = [lax.rem(y + turn(i), 4) for i in range(4)]
    v_copies = []
    for i, q in enumerate(quads):
        rows = pl.ds(pl.multiple_of(q * 256, 256), 256)
        v_copies.append(pltpu.make_async_copy(v_hbm.at[rows, :], v_buf.at[i], v_sem.at[i]))

    barrier = pltpu.get_barrier_semaphore()
    for d in range(1, 8):
        pl.semaphore_signal(barrier, inc=1, device_id=(lax.rem(r + d, 8), c), device_id_type=MESH)
    for d in range(1, 8):
        peer = 2 * lax.rem(chip + d, 8) + core
        pl.semaphore_signal(barrier, inc=1, device_id=(r, peer), device_id_type=MESH)
    sibling = (r, 2 * chip + 1 - core)
    pl.semaphore_signal(barrier, inc=1, device_id=sibling, device_id_type=MESH)
    target = (chip, 2 * lax.rem(r + chip, 8) + core)
    origin = lax.rem(chip + 8 - r, 8)
    moves = (r != 0) | (chip != 0)
    elsewhere = origin != r

    @pl.when(elsewhere)
    def _():
        for k in range(8):
            peer = 2 * k + core
            pl.semaphore_signal(barrier, inc=1, device_id=(origin, peer), device_id_type=MESH)

    for i in range(CHUNKS):
        panel_copies[i].wait()
        if i == CHUNKS - 1:
            for copy in v_copies:
                copy.start()

        def widen(n, _, i=i):
            start = pl.multiple_of(i * piece + n * 64, 64)
            v = panel[pl.ds(start, 64), :].astype(jnp.float32)
            wide[0, pl.ds(8 + start, 64), :] = v[:, :128]
            wide[1, pl.ds(8 + start, 64), :] = v[:, 128:]
            return 0

        lax.fori_loop(0, piece // 64, widen, 0)
    slot_copy.wait()
    sub = lax.broadcasted_iota(jnp.int32, (8, 128), 0)

    def take(g, _):
        base = [3 * slot_ref[g * UNIT + u] + 8 for u in range(UNIT)]
        for h in range(2):
            tiles = []
            for t in range(3 * UNIT // 8):
                tile = None
                for u in range(UNIT):
                    low = 3 * u - 8 * t
                    if low <= -3 or low >= 8:
                        continue
                    v = wide[h, pl.ds(base[u] - low, 8), :]
                    tile = v if tile is None else jnp.where(sub >= low, v, tile)
                tiles.append(tile)
            for t in range(0, len(tiles), 2):
                both = jnp.concatenate([tiles[t], tiles[t + 1]], axis=0).astype(jnp.bfloat16)
                at = pl.multiple_of(g * (3 * UNIT) + t * 8, 16)
                ordered[pl.ds(at, 16), h * 128 : (h + 1) * 128] = both
        return 0

    lax.fori_loop(0, ATOMS // UNIT, take, 0)

    pl.semaphore_wait(barrier, 22)

    def rs_copy(k):
        to_z = lax.rem(z + 1 + lax.rem(k, 2), 2)
        return pltpu.make_async_remote_copy(
            src_ref=sent.at[k], dst_ref=landed.at[k],
            send_sem=rs_send.at[k], recv_sem=rs_recv.at[k],
            device_id=(2 * lax.rem(y + turn(k // 2), 4) + to_z, c), device_id_type=MESH,
        )

    def step(i, _):
        quad, zz = i // 2, lax.rem(i, 2)
        to_z = lax.rem(z + 1 + zz, 2)

        @pl.when(zz == 0)
        def _():
            pltpu.make_async_copy(
                v_hbm.at[pl.ds(0, 256), :], v_buf.at[quad], v_sem.at[quad]
            ).wait()

        rows = pl.ds(pl.multiple_of(to_z * BLOCK, BLOCK), BLOCK)
        part[...] = jnp.dot(
            v_buf[quad, rows, :], ordered[...], preferred_element_type=jnp.float32
        )
        coded, powers = code(part[...].T)
        sent[i, :WIDTH, :] = coded
        sent[i, WIDTH:, :] = powers

        @pl.when(i < 7)
        def _():
            rs_copy(i).start()

        return 0

    lax.fori_loop(0, 8, step, 0)
    rs_copies = [rs_copy(k) for k in range(7)]
    turned = part[...].T
    for k in range(7):
        rs_copies[k].wait_recv()
        turned = turned + decode(landed.at[k])

    own = jnp.sum(turned * turned, axis=0, keepdims=True)
    own_send[...] = jnp.broadcast_to(own, (8, BLOCK))
    pair_copy = pltpu.make_async_remote_copy(
        src_ref=own_send, dst_ref=own_land, send_sem=pair_send, recv_sem=pair_recv,
        device_id=sibling, device_id_type=MESH,
    )
    pair_copy.start()

    t_sent[:WIDTH, :], t_sent[WIDTH:, :] = code(turned)
    t_copy = pltpu.make_async_remote_copy(
        src_ref=t_sent, dst_ref=t_land, send_sem=t_send, recv_sem=t_recv,
        device_id=target, device_id_type=MESH,
    )

    @pl.when(moves)
    def _():
        t_copy.start()

    pair_copy.wait_recv()
    total = own + own_land[0:1, :]
    energy_send[...] = jnp.broadcast_to(total, (8, BLOCK))
    e_copies = [pair_copy]
    own_copies = []
    for d in range(1, 8):
        copy = pltpu.make_async_remote_copy(
            src_ref=energy_send, dst_ref=energy_land.at[d - 1],
            send_sem=e_send.at[d - 1], recv_sem=e_recv.at[d - 1],
            device_id=(r, 2 * lax.rem(chip + d, 8) + core), device_id_type=MESH,
        )
        copy.start()
        own_copies.append(copy)
        to_row_of = lax.rem(r + d, 8)
        copy = pltpu.make_async_remote_copy(
            src_ref=energy_send, dst_ref=there_land.at[chip],
            send_sem=there_send.at[d - 1], recv_sem=there_recv.at[chip],
            device_id=(to_row_of, 2 * lax.rem(to_row_of + r, 8) + core), device_id_type=MESH,
        )
        copy.start()
        e_copies.append(copy)
    e_copies += own_copies
    for d in range(7):
        own_copies[d].wait_recv()
        total = total + energy_land[d, 0:1, :]
    scaled = turned * lax.rsqrt(total / M + epsilon)
    block_n[...] = scaled.T.astype(jnp.bfloat16)

    def rows_of(of_row):
        return pl.ds(pl.multiple_of(of_row * BLOCK, BLOCK), BLOCK)

    def place(of_chip):
        of_row = lax.rem(of_chip + 8 - r, 8)
        return (
            pl.ds(pl.multiple_of(core * WIDTH, WIDTH), WIDTH),
            pl.ds(pl.multiple_of(of_row * BLOCK, BLOCK), BLOCK),
        )

    def to_row(k, src, rows, device):
        copy = pltpu.make_async_remote_copy(
            src_ref=src, dst_ref=col_out.at[rows, :],
            send_sem=c_send.at[k], recv_sem=c_recv.at[k],
            device_id=(device, c), device_id_type=MESH,
        )
        copy.start()
        return copy

    def to_col(k, src, spot, chip_to):
        copy = pltpu.make_async_remote_copy(
            src_ref=src, dst_ref=row_out.at[spot],
            send_sem=b_send.at[k], recv_sem=b_recv.at[k],
            device_id=(r, 2 * chip_to + core), device_id_type=MESH,
        )
        copy.start()
        return copy

    def to_sibling(k, src, spot):
        copy = pltpu.make_async_remote_copy(
            src_ref=src, dst_ref=row_out.at[spot],
            send_sem=s_send.at[k], recv_sem=s_recv.at[k],
            device_id=sibling, device_id_type=MESH,
        )
        copy.start()
        return copy

    c_copies = [to_row(0, block_n, rows_of(r), 2 * y + 1 - z)]
    col_out[rows_of(r), :] = block_n[...]

    there_sum[...] = total

    @pl.when(elsewhere)
    def _():
        energy = jnp.zeros((1, BLOCK), jnp.float32)
        for k in range(8):
            pltpu.make_async_remote_copy(
                src_ref=energy_send, dst_ref=there_land.at[k],
                send_sem=there_send.at[0], recv_sem=there_recv.at[k],
                device_id=target, device_id_type=MESH,
            ).wait_recv()
            energy = energy + there_land[k, 0:1, :]
        there_sum[...] = energy

    @pl.when(moves)
    def _():
        t_copy.wait_recv()
        factor = lax.rsqrt(there_sum[...] / M + epsilon)
        moved[...] = (decode(t_land) * factor).astype(jnp.bfloat16)

    @pl.when(jnp.logical_not(moves))
    def _():
        moved[...] = scaled.astype(jnp.bfloat16)

    far = 4 * (1 - zh)
    near = 4 * zh
    s_copies = [to_sibling(0, moved, place(chip))]
    b_copies = [to_col(0, moved, place(chip), far + x)]
    for d in (2, 1, 3):
        b_copies.append(to_col(d, moved, place(chip), near + lax.rem(x + d, 4)))
    for d in (2, 1, 3):
        c_copies.append(to_row(d, block_n, rows_of(r), 2 * lax.rem(y + d, 4) + z))
    row_out[place(chip)] = moved[...]
    b_copies[0].wait_recv()
    other = place(far + x)
    for d in (2, 1, 3):
        b_copies.append(to_col(3 + d, row_out.at[other], other, near + lax.rem(x + d, 4)))
    c_copies[0].wait_recv()
    beside = rows_of(2 * y + 1 - z)
    for d in (2, 1, 3):
        c_copies.append(to_row(3 + d, col_out.at[beside, :], beside, 2 * lax.rem(y + d, 4) + z))
    s_copies.append(to_sibling(1, row_out.at[other], other))
    for n, side in enumerate((near, far)):
        for m, d in ((1, 1), (2, 3), (0, 2)):
            b_copies[1 + 3 * n + m].wait_recv()
            spot = place(side + lax.rem(x + 4 - d, 4))
            s_copies.append(to_sibling(2 + 3 * n + m, row_out.at[spot], spot))
    for copy in (*s_copies, *c_copies[1:]):
        copy.wait_recv()

    for copy in (*rs_copies, *e_copies, *c_copies, *b_copies, *s_copies):
        copy.wait_send()

    @pl.when(moves)
    def _():
        t_copy.wait_send()


def project(velocities, modes_panel, atom_slot):
    return pl.pallas_call(
        project_kernel,
        out_shape=(
            jax.ShapeDtypeStruct((2 * WIDTH, S), jnp.bfloat16),
            jax.ShapeDtypeStruct((S, WIDTH), jnp.bfloat16),
        ),
        in_specs=[
            pl.BlockSpec(memory_space=pltpu.HBM),
            pl.BlockSpec(memory_space=pltpu.HBM),
            pl.BlockSpec(memory_space=pltpu.HBM),
        ],
        out_specs=(pl.BlockSpec(memory_space=VMEM), pl.BlockSpec(memory_space=VMEM)),
        scratch_shapes=[
            pltpu.SMEM((ATOMS,), jnp.int32),
            VMEM((ROWS, WIDTH), jnp.bfloat16),
            VMEM((2, ROWS + 16, 128), jnp.float32),
            VMEM((ROWS, WIDTH), jnp.bfloat16),
            VMEM((4, 256, ROWS), jnp.bfloat16),
            VMEM((BLOCK, WIDTH), jnp.float32),
            VMEM((8, WIDTH + 16, BLOCK), jnp.int16),
            VMEM((7, WIDTH + 16, BLOCK), jnp.int16),
            VMEM((8, BLOCK), jnp.float32),
            VMEM((8, BLOCK), jnp.float32),
            VMEM((8, BLOCK), jnp.float32),
            VMEM((7, 8, BLOCK), jnp.float32),
            VMEM((8, 8, BLOCK), jnp.float32),
            VMEM((1, BLOCK), jnp.float32),
            VMEM((WIDTH + 16, BLOCK), jnp.int16),
            VMEM((WIDTH + 16, BLOCK), jnp.int16),
            VMEM((BLOCK, WIDTH), jnp.bfloat16),
            VMEM((WIDTH, BLOCK), jnp.bfloat16),
            DMA, DMA((CHUNKS,)), DMA((4,)),
            DMA((7,)), DMA((7,)),
            DMA, DMA,
            DMA((7,)), DMA((7,)),
            DMA((7,)), DMA((8,)),
            DMA((7,)), DMA((7,)),
            DMA, DMA,
            DMA((7,)), DMA((7,)),
            DMA((8,)), DMA((8,)),
        ],
        compiler_params=pltpu.CompilerParams(
            collective_id=0, has_side_effects=True, vmem_limit_bytes=52 * 2**20
        ),
    )(atom_slot, modes_panel, velocities)


def correlate_kernel(lag_ref, rows_ref, cols_ref, out_hbm, padded, shifted, held, out_sem):
    for h in range(2):
        padded[h, :S, :] = cols_ref[:, h * 128 : (h + 1) * 128].astype(jnp.float32)
        padded[h, S:, :] = jnp.zeros((MAXLAG, 128), jnp.float32)
    copies = []
    for i in range(LAGS):
        lag = lag_ref[i]
        for h in range(2):
            cut = padded[h, pl.ds(lag, S), :].astype(jnp.bfloat16)
            shifted[i % 2, :, h * 128 : (h + 1) * 128] = cut
        factor = lax.rsqrt(jnp.broadcast_to((S - lag).astype(jnp.float32), (1, WIDTH)))
        for p in range(2):
            rows = pl.ds(p * WIDTH, WIDTH)
            product = jnp.dot(
                rows_ref[rows, :], shifted[i % 2], preferred_element_type=jnp.float32
            )
            held[i, rows, :] = product * factor
        copies.append(pltpu.make_async_copy(held.at[i], out_hbm.at[i], out_sem.at[i]))
        copies[-1].start()
    for copy in copies:
        copy.wait()


def correlate(row_modes, column_modes, lag_offsets):
    return pl.pallas_call(
        correlate_kernel,
        out_shape=jax.ShapeDtypeStruct((LAGS, 2 * WIDTH, WIDTH), jnp.float32),
        in_specs=[
            pl.BlockSpec(memory_space=pltpu.SMEM),
            pl.BlockSpec(memory_space=VMEM),
            pl.BlockSpec(memory_space=VMEM),
        ],
        out_specs=pl.BlockSpec(memory_space=pl.ANY),
        scratch_shapes=[
            VMEM((2, S + MAXLAG, 128), jnp.float32),
            VMEM((2, S, WIDTH), jnp.bfloat16),
            VMEM((LAGS, 2 * WIDTH, WIDTH), jnp.float32),
            DMA((LAGS,)),
        ],
        compiler_params=pltpu.CompilerParams(vmem_limit_bytes=24 * 2**20),
    )(lag_offsets, row_modes, column_modes)


def local(velocities, modes_panel, atom_slot, lag_offsets):
    row_modes, column_modes = project(velocities, modes_panel, atom_slot)
    return correlate(row_modes, column_modes, lag_offsets)


def solution(mesh):
    return jax.shard_map(
        local,
        mesh=mesh,
        in_specs=(P(None, "row"), P("row", "col"), P("row"), P()),
        out_specs=P(None, "row", "col"),
        check_vma=False,
    )
```

```python
import jax
import jax.numpy as jnp
from jax import lax
from jax.experimental import pallas as pl
from jax.experimental.pallas import tpu as pltpu
from jax.sharding import PartitionSpec as P

M = 4096
LAGS = 8
MAXLAG = 256
S = 1024
ATOMS = 2560
ROWS = 3 * ATOMS
WIDTH = 256
BLOCK = 128
CHUNKS = 8
UNIT = 16
TINY = 1e-30
FULL = 32760.0
epsilon = 1e-06

MESH = pl.DeviceIdType.MESH
VMEM = pltpu.VMEM
DMA = pltpu.SemaphoreType.DMA


def code(values):
    top = jnp.max(jnp.abs(values), axis=0, keepdims=True)
    power = jnp.ceil(jnp.log2(jnp.maximum(top, TINY)))
    coded = jnp.round(values * (FULL * jnp.exp2(-power)))
    powers = jnp.broadcast_to(power, (16, values.shape[1]))
    return coded.astype(jnp.int32).astype(jnp.int16), powers.astype(jnp.int32).astype(jnp.int16)


def decode(ref):
    power = ref[WIDTH:, :].astype(jnp.int32).astype(jnp.float32)[0:1, :]
    return ref[:WIDTH, :].astype(jnp.int32).astype(jnp.float32) * (jnp.exp2(power) / FULL)


def turn(i):
    return jnp.where(i == 3, 0, jnp.where(i == 2, 1, i + 2))


def project_kernel(
    slot_hbm, panel_hbm, v_hbm, row_out, col_out,
    slot_ref, panel, wide, ordered, v_buf, part, sent, landed, own_send, own_land, energy_send, energy_land, there_land, there_sum, t_sent, t_land, block_n, moved,
    slot_sem, panel_sem, v_sem, rs_send, rs_recv, pair_send, pair_recv, e_send, e_recv, there_send, there_recv, c_send, c_recv, t_send, t_recv,
    b_send, b_recv, s_send, s_recv,
):
    r, c = lax.axis_index("row"), lax.axis_index("col")
    y, z = r // 2, r % 2
    chip, core = c // 2, c % 2
    zh, x = chip // 4, chip % 4

    slot_copy = pltpu.make_async_copy(slot_hbm, slot_ref, slot_sem)
    slot_copy.start()
    piece = ROWS // CHUNKS
    panel_copies = []
    for i in range(CHUNKS):
        rows = pl.ds(i * piece, piece)
        panel_copies.append(
            pltpu.make_async_copy(panel_hbm.at[rows, :], panel.at[rows, :], panel_sem.at[i])
        )
        panel_copies[-1].start()
    quads = [lax.rem(y + turn(i), 4) for i in range(4)]
    v_copies = []
    for i, q in enumerate(quads):
        rows = pl.ds(pl.multiple_of(q * 256, 256), 256)
        v_copies.append(pltpu.make_async_copy(v_hbm.at[rows, :], v_buf.at[i], v_sem.at[i]))

    barrier = pltpu.get_barrier_semaphore()
    for d in range(1, 8):
        pl.semaphore_signal(barrier, inc=1, device_id=(lax.rem(r + d, 8), c), device_id_type=MESH)
    for d in range(1, 8):
        peer = 2 * lax.rem(chip + d, 8) + core
        pl.semaphore_signal(barrier, inc=1, device_id=(r, peer), device_id_type=MESH)
    sibling = (r, 2 * chip + 1 - core)
    pl.semaphore_signal(barrier, inc=1, device_id=sibling, device_id_type=MESH)
    target = (chip, 2 * lax.rem(r + chip, 8) + core)
    origin = lax.rem(chip + 8 - r, 8)
    moves = (r != 0) | (chip != 0)
    elsewhere = origin != r

    @pl.when(elsewhere)
    def _():
        for k in range(8):
            peer = 2 * k + core
            pl.semaphore_signal(barrier, inc=1, device_id=(origin, peer), device_id_type=MESH)

    for i in range(CHUNKS):
        panel_copies[i].wait()
        if i == CHUNKS - 1:
            for copy in v_copies:
                copy.start()

        def widen(n, _, i=i):
            start = pl.multiple_of(i * piece + n * 64, 64)
            v = panel[pl.ds(start, 64), :].astype(jnp.float32)
            wide[0, pl.ds(8 + start, 64), :] = v[:, :128]
            wide[1, pl.ds(8 + start, 64), :] = v[:, 128:]
            return 0

        lax.fori_loop(0, piece // 64, widen, 0)
    slot_copy.wait()
    sub = lax.broadcasted_iota(jnp.int32, (8, 128), 0)

    def take(g, _):
        base = [3 * slot_ref[g * UNIT + u] + 8 for u in range(UNIT)]
        for h in range(2):
            tiles = []
            for t in range(3 * UNIT // 8):
                tile = None
                for u in range(UNIT):
                    low = 3 * u - 8 * t
                    if low <= -3 or low >= 8:
                        continue
                    v = wide[h, pl.ds(base[u] - low, 8), :]
                    tile = v if tile is None else jnp.where(sub >= low, v, tile)
                tiles.append(tile)
            for t in range(0, len(tiles), 2):
                both = jnp.concatenate([tiles[t], tiles[t + 1]], axis=0).astype(jnp.bfloat16)
                at = pl.multiple_of(g * (3 * UNIT) + t * 8, 16)
                ordered[pl.ds(at, 16), h * 128 : (h + 1) * 128] = both
        return 0

    lax.fori_loop(0, ATOMS // UNIT, take, 0)

    pl.semaphore_wait(barrier, 22)

    def rs_copy(k):
        to_z = lax.rem(z + 1 + lax.rem(k, 2), 2)
        return pltpu.make_async_remote_copy(
            src_ref=sent.at[k], dst_ref=landed.at[k],
            send_sem=rs_send.at[k], recv_sem=rs_recv.at[k],
            device_id=(2 * lax.rem(y + turn(k // 2), 4) + to_z, c), device_id_type=MESH,
        )

    def step(i, _):
        quad, zz = i // 2, lax.rem(i, 2)
        to_z = lax.rem(z + 1 + zz, 2)

        @pl.when(zz == 0)
        def _():
            pltpu.make_async_copy(
                v_hbm.at[pl.ds(0, 256), :], v_buf.at[quad], v_sem.at[quad]
            ).wait()

        rows = pl.ds(pl.multiple_of(to_z * BLOCK, BLOCK), BLOCK)
        part[...] = jnp.dot(
            v_buf[quad, rows, :], ordered[...], preferred_element_type=jnp.float32
        )
        coded, powers = code(part[...].T)
        sent[i, :WIDTH, :] = coded
        sent[i, WIDTH:, :] = powers

        @pl.when(i < 7)
        def _():
            rs_copy(i).start()

        return 0

    lax.fori_loop(0, 8, step, 0)
    rs_copies = [rs_copy(k) for k in range(7)]
    turned = part[...].T
    for k in range(7):
        rs_copies[k].wait_recv()
        turned = turned + decode(landed.at[k])

    own = jnp.sum(turned * turned, axis=0, keepdims=True)
    own_send[...] = jnp.broadcast_to(own, (8, BLOCK))
    pair_copy = pltpu.make_async_remote_copy(
        src_ref=own_send, dst_ref=own_land, send_sem=pair_send, recv_sem=pair_recv,
        device_id=sibling, device_id_type=MESH,
    )
    pair_copy.start()

    t_sent[:WIDTH, :], t_sent[WIDTH:, :] = code(turned)
    t_copy = pltpu.make_async_remote_copy(
        src_ref=t_sent, dst_ref=t_land, send_sem=t_send, recv_sem=t_recv,
        device_id=target, device_id_type=MESH,
    )

    @pl.when(moves)
    def _():
        t_copy.start()

    pair_copy.wait_recv()
    total = own + own_land[0:1, :]
    energy_send[...] = jnp.broadcast_to(total, (8, BLOCK))
    e_copies = [pair_copy]
    own_copies = []
    for d in range(1, 8):
        copy = pltpu.make_async_remote_copy(
            src_ref=energy_send, dst_ref=energy_land.at[d - 1],
            send_sem=e_send.at[d - 1], recv_sem=e_recv.at[d - 1],
            device_id=(r, 2 * lax.rem(chip + d, 8) + core), device_id_type=MESH,
        )
        copy.start()
        own_copies.append(copy)
        to_row_of = lax.rem(r + d, 8)
        copy = pltpu.make_async_remote_copy(
            src_ref=energy_send, dst_ref=there_land.at[chip],
            send_sem=there_send.at[d - 1], recv_sem=there_recv.at[chip],
            device_id=(to_row_of, 2 * lax.rem(to_row_of + r, 8) + core), device_id_type=MESH,
        )
        copy.start()
        e_copies.append(copy)
    e_copies += own_copies
    for d in range(7):
        own_copies[d].wait_recv()
        total = total + energy_land[d, 0:1, :]
    scaled = turned * lax.rsqrt(total / M + epsilon)
    block_n[...] = scaled.T.astype(jnp.bfloat16)

    def rows_of(of_row):
        return pl.ds(pl.multiple_of(of_row * BLOCK, BLOCK), BLOCK)

    def place(of_chip):
        of_row = lax.rem(of_chip + 8 - r, 8)
        return (
            pl.ds(pl.multiple_of(core * WIDTH, WIDTH), WIDTH),
            pl.ds(pl.multiple_of(of_row * BLOCK, BLOCK), BLOCK),
        )

    def to_row(k, src, rows, device):
        copy = pltpu.make_async_remote_copy(
            src_ref=src, dst_ref=col_out.at[rows, :],
            send_sem=c_send.at[k], recv_sem=c_recv.at[k],
            device_id=(device, c), device_id_type=MESH,
        )
        copy.start()
        return copy

    def to_col(k, src, spot, chip_to):
        copy = pltpu.make_async_remote_copy(
            src_ref=src, dst_ref=row_out.at[spot],
            send_sem=b_send.at[k], recv_sem=b_recv.at[k],
            device_id=(r, 2 * chip_to + core), device_id_type=MESH,
        )
        copy.start()
        return copy

    def to_sibling(k, src, spot):
        copy = pltpu.make_async_remote_copy(
            src_ref=src, dst_ref=row_out.at[spot],
            send_sem=s_send.at[k], recv_sem=s_recv.at[k],
            device_id=sibling, device_id_type=MESH,
        )
        copy.start()
        return copy

    c_copies = [to_row(0, block_n, rows_of(r), 2 * y + 1 - z)]
    col_out[rows_of(r), :] = block_n[...]

    there_sum[...] = total

    @pl.when(elsewhere)
    def _():
        energy = jnp.zeros((1, BLOCK), jnp.float32)
        for k in range(8):
            pltpu.make_async_remote_copy(
                src_ref=energy_send, dst_ref=there_land.at[k],
                send_sem=there_send.at[0], recv_sem=there_recv.at[k],
                device_id=target, device_id_type=MESH,
            ).wait_recv()
            energy = energy + there_land[k, 0:1, :]
        there_sum[...] = energy

    @pl.when(moves)
    def _():
        t_copy.wait_recv()
        factor = lax.rsqrt(there_sum[...] / M + epsilon)
        moved[...] = (decode(t_land) * factor).astype(jnp.bfloat16)

    @pl.when(jnp.logical_not(moves))
    def _():
        moved[...] = scaled.astype(jnp.bfloat16)

    far = 4 * (1 - zh)
    near = 4 * zh
    s_copies = [to_sibling(0, moved, place(chip))]
    b_copies = [to_col(0, moved, place(chip), far + x)]
    for d in (2, 1, 3):
        b_copies.append(to_col(d, moved, place(chip), near + lax.rem(x + d, 4)))
    for d in (2, 1, 3):
        c_copies.append(to_row(d, block_n, rows_of(r), 2 * lax.rem(y + d, 4) + z))
    row_out[place(chip)] = moved[...]
    b_copies[0].wait_recv()
    other = place(far + x)
    for d in (2, 1, 3):
        b_copies.append(to_col(3 + d, row_out.at[other], other, near + lax.rem(x + d, 4)))
    c_copies[0].wait_recv()
    beside = rows_of(2 * y + 1 - z)
    for d in (2, 1, 3):
        c_copies.append(to_row(3 + d, col_out.at[beside, :], beside, 2 * lax.rem(y + d, 4) + z))
    s_copies.append(to_sibling(1, row_out.at[other], other))
    for n, side in enumerate((near, far)):
        for m, d in ((1, 1), (2, 3), (0, 2)):
            b_copies[1 + 3 * n + m].wait_recv()
            spot = place(side + lax.rem(x + 4 - d, 4))
            s_copies.append(to_sibling(2 + 3 * n + m, row_out.at[spot], spot))
    for copy in (*s_copies, *c_copies[1:]):
        copy.wait_recv()

    for copy in (*rs_copies, *e_copies, *c_copies, *b_copies, *s_copies):
        copy.wait_send()

    @pl.when(moves)
    def _():
        t_copy.wait_send()


def project(velocities, modes_panel, atom_slot):
    return pl.pallas_call(
        project_kernel,
        out_shape=(
            jax.ShapeDtypeStruct((2 * WIDTH, S), jnp.bfloat16),
            jax.ShapeDtypeStruct((S, WIDTH), jnp.bfloat16),
        ),
        in_specs=[
            pl.BlockSpec(memory_space=pltpu.HBM),
            pl.BlockSpec(memory_space=pltpu.HBM),
            pl.BlockSpec(memory_space=pltpu.HBM),
        ],
        out_specs=(pl.BlockSpec(memory_space=VMEM), pl.BlockSpec(memory_space=VMEM)),
        scratch_shapes=[
            pltpu.SMEM((ATOMS,), jnp.int32),
            VMEM((ROWS, WIDTH), jnp.bfloat16),
            VMEM((2, ROWS + 16, 128), jnp.float32),
            VMEM((ROWS, WIDTH), jnp.bfloat16),
            VMEM((4, 256, ROWS), jnp.bfloat16),
            VMEM((BLOCK, WIDTH), jnp.float32),
            VMEM((8, WIDTH + 16, BLOCK), jnp.int16),
            VMEM((7, WIDTH + 16, BLOCK), jnp.int16),
            VMEM((8, BLOCK), jnp.float32),
            VMEM((8, BLOCK), jnp.float32),
            VMEM((8, BLOCK), jnp.float32),
            VMEM((7, 8, BLOCK), jnp.float32),
            VMEM((8, 8, BLOCK), jnp.float32),
            VMEM((1, BLOCK), jnp.float32),
            VMEM((WIDTH + 16, BLOCK), jnp.int16),
            VMEM((WIDTH + 16, BLOCK), jnp.int16),
            VMEM((BLOCK, WIDTH), jnp.bfloat16),
            VMEM((WIDTH, BLOCK), jnp.bfloat16),
            DMA, DMA((CHUNKS,)), DMA((4,)),
            DMA((7,)), DMA((7,)),
            DMA, DMA,
            DMA((7,)), DMA((7,)),
            DMA((7,)), DMA((8,)),
            DMA((7,)), DMA((7,)),
            DMA, DMA,
            DMA((7,)), DMA((7,)),
            DMA((8,)), DMA((8,)),
        ],
        compiler_params=pltpu.CompilerParams(
            collective_id=0, has_side_effects=True, vmem_limit_bytes=52 * 2**20
        ),
    )(atom_slot, modes_panel, velocities)


def correlate_kernel(lag_ref, rows_ref, cols_ref, out_hbm, padded, shifted, held, out_sem):
    for h in range(2):
        padded[h, :S, :] = cols_ref[:, h * 128 : (h + 1) * 128].astype(jnp.float32)
        padded[h, S:, :] = jnp.zeros((MAXLAG, 128), jnp.float32)
    copies = []
    for i in range(LAGS):
        lag = lag_ref[i]
        for h in range(2):
            cut = padded[h, pl.ds(lag, S), :].astype(jnp.bfloat16)
            shifted[i % 2, :, h * 128 : (h + 1) * 128] = cut
        factor = lax.rsqrt(jnp.broadcast_to((S - lag).astype(jnp.float32), (1, WIDTH)))
        for p in range(2):
            rows = pl.ds(p * WIDTH, WIDTH)
            product = jnp.dot(
                rows_ref[rows, :], shifted[i % 2], preferred_element_type=jnp.float32
            )
            held[i, rows, :] = product * factor
            copy = pltpu.make_async_copy(
                held.at[i, rows, :], out_hbm.at[i, rows, :], out_sem.at[2 * i + p]
            )
            copy.start()
            copies.append(copy)
    for copy in copies:
        copy.wait()


def correlate(row_modes, column_modes, lag_offsets):
    return pl.pallas_call(
        correlate_kernel,
        out_shape=jax.ShapeDtypeStruct((LAGS, 2 * WIDTH, WIDTH), jnp.float32),
        in_specs=[
            pl.BlockSpec(memory_space=pltpu.SMEM),
            pl.BlockSpec(memory_space=VMEM),
            pl.BlockSpec(memory_space=VMEM),
        ],
        out_specs=pl.BlockSpec(memory_space=pl.ANY),
        scratch_shapes=[
            VMEM((2, S + MAXLAG, 128), jnp.float32),
            VMEM((2, S, WIDTH), jnp.bfloat16),
            VMEM((LAGS, 2 * WIDTH, WIDTH), jnp.float32),
            DMA((2 * LAGS,)),
        ],
        compiler_params=pltpu.CompilerParams(vmem_limit_bytes=24 * 2**20),
    )(lag_offsets, row_modes, column_modes)


def local(velocities, modes_panel, atom_slot, lag_offsets):
    row_modes, column_modes = project(velocities, modes_panel, atom_slot)
    return correlate(row_modes, column_modes, lag_offsets)


def solution(mesh):
    return jax.shard_map(
        local,
        mesh=mesh,
        in_specs=(P(None, "row"), P("row", "col"), P("row"), P()),
        out_specs=P(None, "row", "col"),
        check_vma=False,
    )
```
